32 devices in a mesh: pts: 8 (over z, y), freq: 4 (over x, core).
Axes of the slice: x: 2, y: 2, z: 4, core: 2. Of those that a mesh axis runs over, the one named last changes fastest.
Arguments:
- spectra: bfloat16 [64, 5, 2048, 128], P('freq', None, 'pts'), parts along dimension 0, may hold values from -200 to 200, as said below
- weights: float32 [2048], P('pts'), as said below
Outputs:
- mode_shapes: bfloat16 [64, 5, 2048, 128], P('freq', None, 'pts'), parts along dimension 0
The draws below stay inside these ranges and needn't reach their ends.
There are 4 independent parts, one for each index of `freq`. The reference program is written for one: setup_inputs(seed, part) draws one part's arguments, and reference() takes and returns one part's arrays. A program takes and returns all parts, laid end to end along the dimension named above; an argument that names none is the same for every part. Nothing has to cross between parts.
Inputs may be any that keep to these rules, and one draw needn't show every extreme that they name: `spectra`: each row (frequency, variable, point) and each block's column pair has its own scale; the complex columns are independent. `weights`: Positive; their sum is of order one.
All inputs are finite; a program needn't handle non-finite values.
Results may differ from the reference program's by a relative error of at most 0.0054.
Values sent between devices are 32-bit elements; how exact they have to be, the bound alone decides.
A program may use at most 64 MiB of HBM per device.

```python
import math
import jax
import jax.numpy as jnp
from jax import lax

BLOCKS = 64
VARS = 5
COLS = 128
FREQ_DEV = 16
NS_STEPS = 10
POINTS = 2048


def draw_spectra(key, part):
    key = jax.random.fold_in(key, 11)
    key_base = jax.random.fold_in(key, 1)
    key_cols = jax.random.fold_in(key, 3)
    key_rows = jax.random.fold_in(key, 4)
    shape = (FREQ_DEV, VARS, POINTS, 2 * BLOCKS)
    base = jnp.clip(jax.random.normal(key_base, shape, jnp.float32), -5.0, 5.0)
    row_scale = jnp.exp(jax.random.uniform(key_rows, (FREQ_DEV, VARS, POINTS, 1), jnp.float32, math.log(0.5), math.log(2.0)))
    col_scale = jnp.exp(jax.random.uniform(key_cols, (FREQ_DEV, 1, 1, BLOCKS), jnp.float32, 0.0, math.log(10.0)))
    col_scale = jnp.concatenate([col_scale, col_scale], -1)
    return (base * col_scale * row_scale).astype(jnp.bfloat16)


def draw_weights(key, part):
    key = jax.random.fold_in(key, 23)
    position = jnp.arange(POINTS).astype(jnp.float32) / POINTS
    trend = jnp.exp(math.log(3.0) * position)
    rough = jnp.exp(jax.random.uniform(key, (POINTS,), jnp.float32, math.log(0.5), math.log(2.0)))
    return (trend * rough / POINTS).astype(jnp.float32)


def setup_inputs(seed: int = 0, part: int = 0) -> dict:
    keys = jax.random.split(jax.random.key(seed), 3)
    part_keys = jax.random.split(jax.random.fold_in(keys[2], part), 3)
    return {
        "spectra": draw_spectra(jax.random.fold_in(jax.random.fold_in(keys[2], part), 71), part),
        "weights": draw_weights(jax.random.fold_in(keys[2], 71), part),
    }


def fold_cross(products):
    half_cols = products.shape[-1] // 2
    top_left = products[:half_cols, :half_cols]
    top_right = products[:half_cols, half_cols:]
    bottom_left = products[half_cols:, :half_cols]
    bottom_right = products[half_cols:, half_cols:]
    real_part = top_left + bottom_right
    imag_part = top_right - bottom_left
    upper_row = jnp.concatenate([real_part, imag_part], 1)
    lower_row = jnp.concatenate([-imag_part, real_part], 1)
    return jnp.concatenate([upper_row, lower_row], 0)

def reference(spectra, weights):
    results = []
    root_weights = jnp.sqrt(weights)
    for freq_index in range(FREQ_DEV):
        block = spectra[freq_index]
        weighted = (root_weights[None, :, None] * block.astype(jnp.float32)).astype(jnp.bfloat16)
        flat_rows = weighted.reshape(VARS * POINTS, COLS)
        products = jnp.dot(flat_rows.T.astype(jnp.float32), flat_rows.astype(jnp.float32), preferred_element_type=jnp.float32)
        cross_gram = fold_cross(products)
        upper_factor = jnp.linalg.cholesky(cross_gram).T
        frob_norm = jnp.sqrt(jnp.sum(upper_factor * upper_factor))
        polar = upper_factor / frob_norm
        for sweep in range(NS_STEPS):
            inner_gram = jnp.dot(polar.T, polar, precision=lax.Precision.HIGHEST)
            polar = 1.5 * polar - 0.5 * jnp.dot(polar, inner_gram, precision=lax.Precision.HIGHEST)
        mapping = lax.linalg.triangular_solve(upper_factor, polar, left_side=True, lower=False).astype(jnp.bfloat16)
        source_rows = block.reshape(VARS * POINTS, COLS)
        shapes = jnp.dot(source_rows.astype(jnp.float32), mapping.astype(jnp.float32), preferred_element_type=jnp.float32).astype(jnp.bfloat16)
        results.append(shapes.reshape(VARS, POINTS, COLS))
    return jnp.stack(results, 0)
```

```python
import functools

import jax
import jax.numpy as jnp
from jax import lax
from jax.experimental import pallas as pl
from jax.experimental.pallas import tpu as pltpu
from jax.sharding import PartitionSpec as P

NS_STEPS = 10
MESH = pl.DeviceIdType.MESH


def places(shape):
    return (
        lax.broadcasted_iota(jnp.int32, shape, 0),
        lax.broadcasted_iota(jnp.int32, shape, 1),
    )


def pack(top):
    half, cols = top.shape
    row, lane = places(top.shape)
    left = lane < half
    upper = jnp.where(left, lane, lane - half) >= row
    rolled = pltpu.roll(top, half, 1)
    both = jnp.where(jnp.logical_xor(left, upper), rolled, top)
    quarter = half // 2
    return jnp.where(left[:quarter], both[:quarter], both[quarter:])


def unpack(packed):
    quarter, cols = packed.shape
    half = 2 * quarter
    left = places(packed.shape)[1] < half
    rolled = pltpu.roll(packed, half, 1)
    top = jnp.where(left, packed, rolled)
    bottom = jnp.where(left, rolled, packed)
    full = jnp.concatenate([top, bottom, top, bottom], 0)
    flipped = full.T
    row, lane = places(full.shape)
    row_left, lane_left = row < half, lane < half
    i = jnp.where(row_left, row, row - half)
    j = jnp.where(lane_left, lane, lane - half)
    real = jnp.where(j >= i, full, flipped)
    imag = jnp.where(j < i, full, jnp.where(j > i, -flipped, 0.0))
    imag = jnp.where(row_left, imag, -imag)
    return jnp.where(jnp.logical_xor(row_left, lane_left), imag, real)


def split(a):
    high = a.astype(jnp.bfloat16)
    low = (a - high.astype(jnp.float32)).astype(jnp.bfloat16)
    return high, low


def left_form(a):
    high, low = split(a)
    return jnp.concatenate([high, low], 1)


def right_form(b):
    high, low = split(b)
    wide = jnp.concatenate([high, low], 1)
    return jnp.concatenate([wide, wide], 0)


def product(a, b):
    wide = jnp.dot(a, b, preferred_element_type=jnp.float32)
    cols = wide.shape[1] // 2
    return wide[:, :cols] + wide[:, cols:]


def polar_map(crosses):
    order = crosses[0].shape[0]
    row, lane = places((order, order))
    eye = row == lane
    traces = [jnp.sum(jnp.where(eye, c, 0.0), keepdims=True) for c in crosses]
    grams = [c / t for c, t in zip(crosses, traces)]
    maps = [None] * len(crosses)
    for step in range(NS_STEPS):
        factors = [jnp.where(eye, 1.5 - 0.5 * g, -0.5 * g) for g in grams]
        rights = [right_form(m) for m in factors]
        if step < NS_STEPS - 1:
            halves = [product(left_form(g), r) for g, r in zip(grams, rights)]
            grams = [product(left_form(t), r) for t, r in zip(halves, rights)]
        if step == 0:
            maps = factors
        else:
            maps = [product(left_form(q), r) for q, r in zip(maps, rights)]
    return [q * lax.rsqrt(t) for q, t in zip(maps, traces)]


def map_kernel(
    n, spectra, weights, out, held, root, sums_out, sums_in, maps_out, maps_in,
    load_sem, sum_send, sum_recv, map_send, map_recv,
):
    me = lax.axis_index("pts")
    _, group, var_count, points, cols = held.shape
    half = cols // 2
    quarter = half // 2

    def peer(k):
        return lax.rem(me + 1 + k, n)

    def source(k):
        return lax.rem(me + (n - 1) - k, n)

    def load(k):
        return pltpu.make_async_copy(
            spectra.at[pl.ds(peer(k) * group, group)], held.at[k], load_sem.at[k]
        )

    def sum_copy(k):
        return pltpu.make_async_remote_copy(
            src_ref=sums_out.at[k], dst_ref=sums_in.at[k], send_sem=sum_send.at[k],
            recv_sem=sum_recv.at[k], device_id={"pts": peer(k)}, device_id_type=MESH,
        )

    def map_copy(k):
        return pltpu.make_async_remote_copy(
            src_ref=maps_out, dst_ref=maps_in.at[k], send_sem=map_send.at[k],
            recv_sem=map_recv.at[k], device_id={"pts": peer(k)}, device_id_type=MESH,
        )

    barrier = pltpu.get_barrier_semaphore()
    for k in range(n - 1):
        pl.semaphore_signal(barrier, inc=1, device_id={"pts": peer(k)}, device_id_type=MESH)
    load(n - 1).start()
    for k in range(n - 1):
        load(k).start()
    root[...] = jnp.broadcast_to(jnp.sqrt(weights[...]), (cols, points)).T

    def packed_sums(k, j):
        total = jnp.zeros((cols, cols), jnp.float32)
        for v in range(var_count):
            rows = (held[k, j, v].astype(jnp.float32) * root[...]).astype(jnp.bfloat16)
            total = total + lax.dot_general(
                rows, rows, (((0,), (0,)), ((), ())), preferred_element_type=jnp.float32
            )
        top, bottom = total[:half], pltpu.roll(total[half:], half, 1)
        lane = places(top.shape)[1]
        return pack(top + jnp.where(lane < half, bottom, -bottom))

    load(n - 1).wait()
    own = [packed_sums(n - 1, j) for j in range(group)]
    pl.semaphore_wait(barrier, n - 1)

    @pl.loop(0, n - 1)
    def _(k):
        load(k).wait()
        for j in range(group):
            sums_out[k, pl.ds(j * quarter, quarter)] = packed_sums(k, j)
        sum_copy(k).start()

    for k in range(n - 1):
        sum_copy(k).wait_recv()
        for j in range(group):
            own[j] = own[j] + sums_in[k, pl.ds(j * quarter, quarter)]

    maps = polar_map([unpack(o) for o in own])
    for j in range(group):
        maps_out[pl.ds(j * quarter, quarter)] = pack(maps[j][:half])
    for k in range(n - 1):
        map_copy(k).start()
    for j in range(group):
        out[me * group + j] = maps[j].astype(out.dtype)

    @pl.loop(0, n - 1)
    def _(k):
        map_copy(k).wait_recv()
        for j in range(group):
            full = unpack(maps_in[k, pl.ds(j * quarter, quarter)])
            out[source(k) * group + j] = full.astype(out.dtype)

    @pl.loop(0, n - 1)
    def _(k):
        sum_copy(k).wait_send()
        map_copy(k).wait_send()


def shape_kernel(spectra, mapping, out):
    pair, var_count, points, cols = spectra.shape
    if pair == 1:
        right = mapping[0]
    else:
        zero = jnp.zeros((cols, cols), mapping.dtype)
        right = jnp.concatenate(
            [
                jnp.concatenate([mapping[0], zero], 1),
                jnp.concatenate([zero, mapping[1]], 1),
            ],
            0,
        )
    for v in range(var_count):
        left = jnp.concatenate([spectra[f, v] for f in range(pair)], 1)
        result = jnp.dot(left, right, preferred_element_type=jnp.float32).astype(out.dtype)
        for f in range(pair):
            out[f, v] = result[:, f * cols : (f + 1) * cols]


def local(n, spectra, weights):
    freq_count, var_count, points, cols = spectra.shape
    group = freq_count // n
    quarter = cols // 4
    mapping = pl.pallas_call(
        functools.partial(map_kernel, n),
        out_shape=jax.ShapeDtypeStruct((freq_count, cols, cols), jnp.bfloat16),
        in_specs=[
            pl.BlockSpec(memory_space=pl.ANY),
            pl.BlockSpec(memory_space=pltpu.VMEM),
        ],
        out_specs=pl.BlockSpec(memory_space=pltpu.VMEM),
        scratch_shapes=[
            pltpu.VMEM((n, group, var_count, points, cols), jnp.bfloat16),
            pltpu.VMEM((points, cols), jnp.float32),
            pltpu.VMEM((n - 1, group * quarter, cols), jnp.float32),
            pltpu.VMEM((n - 1, group * quarter, cols), jnp.float32),
            pltpu.VMEM((group * quarter, cols), jnp.float32),
            pltpu.VMEM((n - 1, group * quarter, cols), jnp.float32),
            pltpu.SemaphoreType.DMA((n,)),
            pltpu.SemaphoreType.DMA((n - 1,)),
            pltpu.SemaphoreType.DMA((n - 1,)),
            pltpu.SemaphoreType.DMA((n - 1,)),
            pltpu.SemaphoreType.DMA((n - 1,)),
        ],
        compiler_params=pltpu.CompilerParams(
            collective_id=0, has_side_effects=True, vmem_limit_bytes=32 * 1024 * 1024
        ),
        name="polar_mapping",
    )(spectra, weights.reshape(1, points))
    pair = 2 if freq_count % 2 == 0 else 1
    block = pl.BlockSpec((pair, var_count, points, cols), lambda f: (f, 0, 0, 0))
    return pl.pallas_call(
        shape_kernel,
        grid=(freq_count // pair,),
        out_shape=jax.ShapeDtypeStruct(spectra.shape, jnp.bfloat16),
        in_specs=[block, pl.BlockSpec((pair, cols, cols), lambda f: (f, 0, 0))],
        out_specs=block,
        compiler_params=pltpu.CompilerParams(vmem_limit_bytes=32 * 1024 * 1024),
        name="mode_shapes",
    )(spectra, mapping)


def solution(mesh):
    in_specs = (P("freq", None, "pts", None), P("pts"))
    out_specs = P("freq", None, "pts", None)
    return jax.shard_map(
        functools.partial(local, mesh.shape["pts"]),
        mesh=mesh, in_specs=in_specs, out_specs=out_specs, check_vma=False,
    )
```

```python
import functools

import jax
import jax.numpy as jnp
from jax import lax
from jax.experimental import pallas as pl
from jax.experimental.pallas import tpu as pltpu
from jax.sharding import PartitionSpec as P

NS_STEPS = 10
MESH = pl.DeviceIdType.MESH


def places(shape):
    return (
        lax.broadcasted_iota(jnp.int32, shape, 0),
        lax.broadcasted_iota(jnp.int32, shape, 1),
    )


def pack(top):
    half, cols = top.shape
    row, lane = places(top.shape)
    left = lane < half
    upper = jnp.where(left, lane, lane - half) >= row
    rolled = pltpu.roll(top, half, 1)
    both = jnp.where(jnp.logical_xor(left, upper), rolled, top)
    quarter = half // 2
    return jnp.where(left[:quarter], both[:quarter], both[quarter:])


def unpack(packed):
    quarter, cols = packed.shape
    half = 2 * quarter
    left = places(packed.shape)[1] < half
    rolled = pltpu.roll(packed, half, 1)
    top = jnp.where(left, packed, rolled)
    bottom = jnp.where(left, rolled, packed)
    full = jnp.concatenate([top, bottom, top, bottom], 0)
    flipped = full.T
    row, lane = places(full.shape)
    row_left, lane_left = row < half, lane < half
    i = jnp.where(row_left, row, row - half)
    j = jnp.where(lane_left, lane, lane - half)
    real = jnp.where(j >= i, full, flipped)
    imag = jnp.where(j < i, full, jnp.where(j > i, -flipped, 0.0))
    imag = jnp.where(row_left, imag, -imag)
    return jnp.where(jnp.logical_xor(row_left, lane_left), imag, real)


def split(a):
    high = a.astype(jnp.bfloat16)
    low = (a - high.astype(jnp.float32)).astype(jnp.bfloat16)
    return high, low


def left_form(a):
    return jnp.concatenate(split(a), 1)


def product(left, right):
    wide = jnp.dot(left, right, preferred_element_type=jnp.float32)
    cols = wide.shape[1] // 2
    return wide[:, :cols] + wide[:, cols:]


def polar_map(crosses):
    order = crosses[0].shape[0]
    row, lane = places((order, order))
    eye = row == lane
    traces = [jnp.sum(jnp.where(eye, c, 0.0), keepdims=True) for c in crosses]
    grams = [c / t for c, t in zip(crosses, traces)]
    maps = [jnp.where(eye, 1.5 - 0.5 * g, -0.5 * g) for g in grams]
    for step in range(NS_STEPS):
        lefts = [left_form(g) for g in grams]
        rights = [jnp.concatenate([g, g], 0) for g in lefts]
        if step == 0:
            squares = [product(g, r) for g, r in zip(lefts, rights)]
        elif step < NS_STEPS - 1:
            both = [
                product(jnp.concatenate([g, left_form(q)], 0), r)
                for g, q, r in zip(lefts, maps, rights)
            ]
            squares = [x[:order] for x in both]
            maps = [1.5 * q - 0.5 * x[order:] for q, x in zip(maps, both)]
        else:
            maps = [1.5 * q - 0.5 * product(left_form(q), r) for q, r in zip(maps, rights)]
        if step < NS_STEPS - 1:
            halves = [1.5 * g - 0.5 * x for g, x in zip(grams, squares)]
            grams = [
                1.5 * t - 0.5 * product(left_form(t), r) for t, r in zip(halves, rights)
            ]
    return [q * lax.rsqrt(t) for q, t in zip(maps, traces)]


def main_kernel(
    n, spectra, weights, out, held, row_weights, root, pair_out, pair_in, sums_out, sums_in,
    maps_out, maps_in, maps_pair, load_sem, weight_sem, pair_send, pair_recv, sum_send, sum_recv,
    map_send, map_recv, fwd_send, fwd_recv,
):
    major = n // 2
    me = lax.axis_index("pts")
    a, b = me // 2, lax.rem(me, 2)
    other = 1 - b
    partner = a * 2 + other
    _, var_count, points, cols = held.shape
    group = held.shape[0] // n
    half = cols // 2
    quarter = half // 2

    def ahead(d):
        return lax.rem(a + d, major)

    def behind(d):
        return lax.rem(a + major - d, major)

    def load(d, side):
        start = (ahead(d) * 2 + (b if side == 0 else other)) * group
        rows = pl.ds(start, group)
        return pltpu.make_async_copy(spectra.at[rows], held.at[rows], load_sem.at[side, d])

    def send(src, dst, send_sem, recv_sem, target):
        return pltpu.make_async_remote_copy(
            src_ref=src, dst_ref=dst, send_sem=send_sem, recv_sem=recv_sem,
            device_id={"pts": target}, device_id_type=MESH,
        )

    def pair_copy(d):
        return send(pair_out.at[d], pair_in.at[d], pair_send.at[d], pair_recv.at[d], partner)

    def sum_copy(d):
        return send(
            sums_out.at[d - 1], sums_in.at[d - 1], sum_send.at[d - 1], sum_recv.at[d - 1],
            ahead(d) * 2 + b,
        )

    def map_copy(d):
        return send(
            maps_out, maps_in.at[d - 1], map_send.at[d - 1], map_recv.at[d - 1], ahead(d) * 2 + b
        )

    def fwd_copy(d):
        src = maps_out if isinstance(d, int) and d == 0 else maps_in.at[d - 1]
        return send(src, maps_pair.at[d], fwd_send.at[d], fwd_recv.at[d], partner)

    barrier = pltpu.get_barrier_semaphore()
    pl.semaphore_signal(barrier, inc=1, device_id={"pts": partner}, device_id_type=MESH)
    for d in range(1, major):
        pl.semaphore_signal(
            barrier, inc=1, device_id={"pts": ahead(d) * 2 + b}, device_id_type=MESH
        )
    weight_copy = pltpu.make_async_copy(weights, row_weights, weight_sem)
    weight_copy.start()
    load(0, 0).start()
    for side in (1, 0):
        for d in range(1, major):
            load(d, side).start()
        if side == 1:
            load(0, 1).start()
    weight_copy.wait()
    root[...] = jnp.broadcast_to(jnp.sqrt(row_weights[...]), (cols, points)).T

    def packed_sums(freq):
        total = jnp.zeros((cols, cols), jnp.float32)
        for v in range(var_count):
            rows = (held[freq, v].astype(jnp.float32) * root[...]).astype(jnp.bfloat16)
            total = total + lax.dot_general(
                rows, rows, (((0,), (0,)), ((), ())), preferred_element_type=jnp.float32
            )
        top, bottom = total[:half], pltpu.roll(total[half:], half, 1)
        lane = places(top.shape)[1]
        return pack(top + jnp.where(lane < half, bottom, -bottom))

    def part(j):
        return pl.ds(j * quarter, quarter)

    def apply(owner, maps):
        first = owner * group
        if group == 2:
            zero = jnp.zeros((cols, cols), jnp.bfloat16)
            right = jnp.concatenate(
                [
                    jnp.concatenate([maps[0], zero], 1),
                    jnp.concatenate([zero, maps[1]], 1),
                ],
                0,
            )
            for v in range(var_count):
                left = jnp.concatenate([held[first, v], held[first + 1, v]], 1)
                wide = jnp.dot(left, right, preferred_element_type=jnp.float32)
                wide = wide.astype(out.dtype)
                out[first, v] = wide[:, :cols]
                out[first + 1, v] = wide[:, cols:]
        else:
            for j in range(group):
                for v in range(var_count):
                    out[first + j, v] = jnp.dot(
                        held[first + j, v], maps[j], preferred_element_type=jnp.float32
                    ).astype(out.dtype)

    load(0, 0).wait()
    own = [packed_sums(me * group + j) for j in range(group)]
    pl.semaphore_wait(barrier, major)

    @pl.loop(0, major)
    def _(i):
        d = lax.rem(i + 1, major)
        load(d, 1).wait()
        for j in range(group):
            pair_out[d, part(j)] = packed_sums((ahead(d) * 2 + other) * group + j)
        pair_copy(d).start()

    @pl.loop(1, major)
    def _(d):
        load(d, 0).wait()
        sums = [packed_sums((ahead(d) * 2 + b) * group + j) for j in range(group)]
        pair_copy(d).wait_recv()
        for j in range(group):
            sums_out[d - 1, part(j)] = sums[j] + pair_in[d, part(j)]
        sum_copy(d).start()

    pair_copy(0).wait_recv()
    for j in range(group):
        own[j] = own[j] + pair_in[0, part(j)]
    for d in range(1, major):
        sum_copy(d).wait_recv()
        for j in range(group):
            own[j] = own[j] + sums_in[d - 1, part(j)]

    maps = polar_map([unpack(o) for o in own])
    for j in range(group):
        maps_out[part(j)] = pack(maps[j][:half])
    for d in range(1, major):
        map_copy(d).start()
    fwd_copy(0).start()
    apply(me, [m.astype(jnp.bfloat16) for m in maps])

    @pl.loop(1, major)
    def _(d):
        map_copy(d).wait_recv()
        fwd_copy(d).start()
        apply(
            behind(d) * 2 + b,
            [unpack(maps_in[d - 1, part(j)]).astype(jnp.bfloat16) for j in range(group)],
        )

    @pl.loop(0, major)
    def _(d):
        send(maps_out, maps_pair.at[d], fwd_send.at[d], fwd_recv.at[d], partner).wait_recv()
        apply(
            behind(d) * 2 + other,
            [unpack(maps_pair[d, part(j)]).astype(jnp.bfloat16) for j in range(group)],
        )

    for d in range(major):
        pair_copy(d).wait_send()
        fwd_copy(d).wait_send()
        if d > 0:
            sum_copy(d).wait_send()
            map_copy(d).wait_send()


def store_kernel(shapes, out, sems):
    copies = [
        pltpu.make_async_copy(shapes.at[f], out.at[f], sems.at[f]) for f in range(shapes.shape[0])
    ]
    for copy in copies:
        copy.start()
    for copy in copies:
        copy.wait()


def local(n, spectra, weights):
    freq_count, var_count, points, cols = spectra.shape
    block = (freq_count // n * (cols // 4), cols)
    major = n // 2
    dma = pltpu.SemaphoreType.DMA
    shapes = pl.pallas_call(
        functools.partial(main_kernel, n),
        out_shape=jax.ShapeDtypeStruct(spectra.shape, jnp.bfloat16),
        in_specs=[pl.BlockSpec(memory_space=pltpu.HBM)] * 2,
        out_specs=pl.BlockSpec(memory_space=pltpu.VMEM),
        scratch_shapes=[
            pltpu.VMEM(spectra.shape, jnp.bfloat16),
            pltpu.VMEM((1, points), jnp.float32),
            pltpu.VMEM((points, cols), jnp.float32),
            pltpu.VMEM((major, *block), jnp.float32),
            pltpu.VMEM((major, *block), jnp.float32),
            pltpu.VMEM((major - 1, *block), jnp.float32),
            pltpu.VMEM((major - 1, *block), jnp.float32),
            pltpu.VMEM(block, jnp.float32),
            pltpu.VMEM((major - 1, *block), jnp.float32),
            pltpu.VMEM((major, *block), jnp.float32),
            dma((2, major)),
            dma,
            dma((major,)),
            dma((major,)),
            dma((major - 1,)),
            dma((major - 1,)),
            dma((major - 1,)),
            dma((major - 1,)),
            dma((major,)),
            dma((major,)),
        ],
        compiler_params=pltpu.CompilerParams(
            collective_id=0, has_side_effects=True, vmem_limit_bytes=32 * 1024 * 1024
        ),
        name="polar_shapes",
    )(
        pltpu.with_memory_space_constraint(spectra, pltpu.HBM),
        pltpu.with_memory_space_constraint(weights.reshape(1, points), pltpu.HBM),
    )
    return pl.pallas_call(
        store_kernel,
        out_shape=jax.ShapeDtypeStruct(spectra.shape, jnp.bfloat16),
        in_specs=[pl.BlockSpec(memory_space=pltpu.VMEM)],
        out_specs=pl.BlockSpec(memory_space=pltpu.HBM),
        scratch_shapes=[dma((freq_count,))],
        compiler_params=pltpu.CompilerParams(vmem_limit_bytes=32 * 1024 * 1024),
        name="store_shapes",
    )(shapes)


def solution(mesh):
    in_specs = (P("freq", None, "pts", None), P("pts"))
    out_specs = P("freq", None, "pts", None)
    return jax.shard_map(
        functools.partial(local, mesh.shape["pts"]),
        mesh=mesh, in_specs=in_specs, out_specs=out_specs, check_vma=False,
    )
```

```python
import functools

import jax
import jax.numpy as jnp
from jax import lax
from jax.experimental import pallas as pl
from jax.experimental.pallas import tpu as pltpu
from jax.sharding import PartitionSpec as P

NS_STEPS = 10
MESH = pl.DeviceIdType.MESH


def places(shape):
    return (
        lax.broadcasted_iota(jnp.int32, shape, 0),
        lax.broadcasted_iota(jnp.int32, shape, 1),
    )


def pack(top):
    half, cols = top.shape
    row, lane = places(top.shape)
    left = lane < half
    upper = jnp.where(left, lane, lane - half) >= row
    rolled = pltpu.roll(top, half, 1)
    both = jnp.where(jnp.logical_xor(left, upper), rolled, top)
    quarter = half // 2
    return jnp.where(left[:quarter], both[:quarter], both[quarter:])


def unpack(packed):
    quarter, cols = packed.shape
    half = 2 * quarter
    left = places(packed.shape)[1] < half
    rolled = pltpu.roll(packed, half, 1)
    top = jnp.where(left, packed, rolled)
    bottom = jnp.where(left, rolled, packed)
    full = jnp.concatenate([top, bottom, top, bottom], 0)
    flipped = full.T
    row, lane = places(full.shape)
    row_left, lane_left = row < half, lane < half
    i = jnp.where(row_left, row, row - half)
    j = jnp.where(lane_left, lane, lane - half)
    real = jnp.where(j >= i, full, flipped)
    imag = jnp.where(j < i, full, jnp.where(j > i, -flipped, 0.0))
    imag = jnp.where(row_left, imag, -imag)
    return jnp.where(jnp.logical_xor(row_left, lane_left), imag, real)


def split(a):
    high = a.astype(jnp.bfloat16)
    low = (a - high.astype(jnp.float32)).astype(jnp.bfloat16)
    return high, low


def left_form(a):
    return jnp.concatenate(split(a), 1)


def product(left, right):
    wide = jnp.dot(left, right, preferred_element_type=jnp.float32)
    cols = wide.shape[1] // 2
    return wide[:, :cols] + wide[:, cols:]


def polar_map(crosses):
    order = crosses[0].shape[0]
    row, lane = places((order, order))
    eye = row == lane
    traces = [jnp.sum(jnp.where(eye, c, 0.0), keepdims=True) for c in crosses]
    grams = [c / t for c, t in zip(crosses, traces)]
    maps = [jnp.where(eye, 1.5 - 0.5 * g, -0.5 * g) for g in grams]
    for step in range(NS_STEPS):
        lefts = [left_form(g) for g in grams]
        rights = [jnp.concatenate([g, g], 0) for g in lefts]
        if step == 0:
            squares = [product(g, r) for g, r in zip(lefts, rights)]
        elif step < NS_STEPS - 1:
            both = [
                product(jnp.concatenate([g, left_form(q)], 0), r)
                for g, q, r in zip(lefts, maps, rights)
            ]
            squares = [x[:order] for x in both]
            maps = [1.5 * q - 0.5 * x[order:] for q, x in zip(maps, both)]
        else:
            maps = [1.5 * q - 0.5 * product(left_form(q), r) for q, r in zip(maps, rights)]
        if step < NS_STEPS - 1:
            halves = [1.5 * g - 0.5 * x for g, x in zip(grams, squares)]
            grams = [
                1.5 * t - 0.5 * product(left_form(t), r) for t, r in zip(halves, rights)
            ]
    return [q * lax.rsqrt(t) for q, t in zip(maps, traces)]


def apply(held, first, maps, out, place):
    group = len(maps)
    _, var_count, points, cols = held.shape
    maps = [m.astype(jnp.bfloat16) for m in maps]
    if group == 2:
        zero = jnp.zeros((cols, cols), jnp.bfloat16)
        right = jnp.concatenate(
            [
                jnp.concatenate([maps[0], zero], 1),
                jnp.concatenate([zero, maps[1]], 1),
            ],
            0,
        )
        for v in range(var_count):
            left = jnp.concatenate([held[first, v], held[first + 1, v]], 1)
            wide = jnp.dot(left, right, preferred_element_type=jnp.float32).astype(out.dtype)
            out[place, v] = wide[:, :cols]
            out[place + 1, v] = wide[:, cols:]
    else:
        for j in range(group):
            for v in range(var_count):
                out[place + j, v] = jnp.dot(
                    held[first + j, v], maps[j], preferred_element_type=jnp.float32
                ).astype(out.dtype)


def main_kernel(
    n, spectra, weights, out, held, maps_pair, row_weights, root, pair_out, pair_in, sums_out,
    sums_in, maps_out, maps_in, load_sem, weight_sem, pair_send, pair_recv, sum_send, sum_recv,
    map_send, map_recv, fwd_send, fwd_recv,
):
    major = n // 2
    me = lax.axis_index("pts")
    a, b = me // 2, lax.rem(me, 2)
    other = 1 - b
    partner = a * 2 + other
    _, var_count, points, cols = held.shape
    group = held.shape[0] // n
    half = cols // 2
    quarter = half // 2

    def ahead(d):
        return lax.rem(a + d, major)

    def behind(d):
        return lax.rem(a + major - d, major)

    def load(d, side):
        start = (ahead(d) * 2 + (b if side == 0 else other)) * group
        rows = pl.ds(start, group)
        return pltpu.make_async_copy(spectra.at[rows], held.at[rows], load_sem.at[side, d])

    def send(src, dst, send_sem, recv_sem, target):
        return pltpu.make_async_remote_copy(
            src_ref=src, dst_ref=dst, send_sem=send_sem, recv_sem=recv_sem,
            device_id={"pts": target}, device_id_type=MESH,
        )

    def pair_copy(d):
        return send(pair_out.at[d], pair_in.at[d], pair_send.at[d], pair_recv.at[d], partner)

    def sum_copy(d):
        return send(
            sums_out.at[d - 1], sums_in.at[d - 1], sum_send.at[d - 1], sum_recv.at[d - 1],
            ahead(d) * 2 + b,
        )

    def map_copy(d):
        return send(
            maps_out, maps_in.at[d - 1], map_send.at[d - 1], map_recv.at[d - 1], ahead(d) * 2 + b
        )

    def fwd_copy(d):
        src = maps_out if isinstance(d, int) and d == 0 else maps_in.at[d - 1]
        return send(src, maps_pair.at[d], fwd_send.at[d], fwd_recv.at[d], partner)

    barrier = pltpu.get_barrier_semaphore()
    pl.semaphore_signal(barrier, inc=1, device_id={"pts": partner}, device_id_type=MESH)
    for d in range(1, major):
        pl.semaphore_signal(
            barrier, inc=1, device_id={"pts": ahead(d) * 2 + b}, device_id_type=MESH
        )
    weight_copy = pltpu.make_async_copy(weights, row_weights, weight_sem)
    weight_copy.start()
    for side in (1, 0):
        for d in range(1, major + 1):
            load(d % major, side).start()
    weight_copy.wait()
    root[...] = jnp.broadcast_to(jnp.sqrt(row_weights[...]), (cols, points)).T

    def packed_sums(freq):
        rows = (held[freq].astype(jnp.float32) * root[...]).astype(jnp.bfloat16)
        rows = rows.reshape(var_count * points, cols)
        total = lax.dot_general(
            rows, rows, (((0,), (0,)), ((), ())), preferred_element_type=jnp.float32
        )
        top, bottom = total[:half], pltpu.roll(total[half:], half, 1)
        lane = places(top.shape)[1]
        return pack(top + jnp.where(lane < half, bottom, -bottom))

    def part(j):
        return pl.ds(j * quarter, quarter)

    def pair_sums(d):
        load(d, 1).wait()
        for j in range(group):
            pair_out[d, part(j)] = packed_sums((ahead(d) * 2 + other) * group + j)

    early = min(2, major)

    @pl.loop(0, early)
    def _(i):
        pair_sums(lax.rem(i + 1, major))

    pl.semaphore_wait(barrier, major)
    for i in range(early):
        pair_copy((i + 1) % major).start()

    @pl.loop(early, major)
    def _(i):
        d = lax.rem(i + 1, major)
        pair_sums(d)
        pair_copy(d).start()

    @pl.loop(1, major)
    def _(d):
        load(d, 0).wait()
        sums = [packed_sums((ahead(d) * 2 + b) * group + j) for j in range(group)]
        pair_copy(d).wait_recv()
        for j in range(group):
            sums_out[d - 1, part(j)] = sums[j] + pair_in[d, part(j)]
        sum_copy(d).start()

    load(0, 0).wait()
    own = [packed_sums(me * group + j) for j in range(group)]
    pair_copy(0).wait_recv()
    for j in range(group):
        own[j] = own[j] + pair_in[0, part(j)]
    for d in range(1, major):
        sum_copy(d).wait_recv()
        for j in range(group):
            own[j] = own[j] + sums_in[d - 1, part(j)]

    maps = polar_map([unpack(o) for o in own])
    for j in range(group):
        maps_out[part(j)] = pack(maps[j][:half])
    for d in range(1, major):
        map_copy(d).start()
    fwd_copy(0).start()
    apply(held, me * group, maps, out, me * group)

    @pl.loop(1, major)
    def _(d):
        map_copy(d).wait_recv()
        fwd_copy(d).start()
        first = (behind(d) * 2 + b) * group
        apply(held, first, [unpack(maps_in[d - 1, part(j)]) for j in range(group)], out, first)

    @pl.loop(0, major)
    def _(d):
        send(maps_out, maps_pair.at[d], fwd_send.at[d], fwd_recv.at[d], partner).wait_recv()

    for d in range(major):
        pair_copy(d).wait_send()
        fwd_copy(d).wait_send()
        if d > 0:
            sum_copy(d).wait_send()
            map_copy(d).wait_send()


def finish_kernel(n, shapes, held, maps_pair, out, late, early_sem, late_sem):
    major = n // 2
    me = lax.axis_index("pts")
    a, b = me // 2, lax.rem(me, 2)
    group = held.shape[0] // n
    quarter = maps_pair.shape[1] // group

    def early_copy(d):
        rows = pl.ds((lax.rem(a + major - d, major) * 2 + b) * group, group)
        return pltpu.make_async_copy(shapes.at[rows], out.at[rows], early_sem.at[d])

    def late_first(d):
        return (lax.rem(a + major - d, major) * 2 + 1 - b) * group

    def late_copy(d):
        return pltpu.make_async_copy(
            late.at[pl.ds(d * group, group)],
            out.at[pl.ds(late_first(d), group)],
            late_sem.at[d],
        )

    for d in range(major):
        early_copy(d).start()

    @pl.loop(0, major)
    def _(d):
        maps = [unpack(maps_pair[d, pl.ds(j * quarter, quarter)]) for j in range(group)]
        apply(held, late_first(d), maps, late, d * group)
        late_copy(d).start()

    for d in range(major):
        early_copy(d).wait()
        late_copy(d).wait()


def local(n, spectra, weights):
    freq_count, var_count, points, cols = spectra.shape
    block = (freq_count // n * (cols // 4), cols)
    major = n // 2
    dma = pltpu.SemaphoreType.DMA
    shapes, held, maps_pair = pl.pallas_call(
        functools.partial(main_kernel, n),
        out_shape=[
            jax.ShapeDtypeStruct(spectra.shape, jnp.bfloat16),
            jax.ShapeDtypeStruct(spectra.shape, jnp.bfloat16),
            jax.ShapeDtypeStruct((major, *block), jnp.float32),
        ],
        in_specs=[pl.BlockSpec(memory_space=pltpu.HBM)] * 2,
        out_specs=[pl.BlockSpec(memory_space=pltpu.VMEM)] * 3,
        scratch_shapes=[
            pltpu.VMEM((1, points), jnp.float32),
            pltpu.VMEM((points, cols), jnp.float32),
            pltpu.VMEM((major, *block), jnp.float32),
            pltpu.VMEM((major, *block), jnp.float32),
            pltpu.VMEM((major - 1, *block), jnp.float32),
            pltpu.VMEM((major - 1, *block), jnp.float32),
            pltpu.VMEM(block, jnp.float32),
            pltpu.VMEM((major - 1, *block), jnp.float32),
            dma((2, major)),
            dma,
            dma((major,)),
            dma((major,)),
            dma((major - 1,)),
            dma((major - 1,)),
            dma((major - 1,)),
            dma((major - 1,)),
            dma((major,)),
            dma((major,)),
        ],
        compiler_params=pltpu.CompilerParams(
            collective_id=0, has_side_effects=True, vmem_limit_bytes=32 * 1024 * 1024
        ),
        name="polar_shapes",
    )(
        pltpu.with_memory_space_constraint(spectra, pltpu.HBM),
        pltpu.with_memory_space_constraint(weights.reshape(1, points), pltpu.HBM),
    )
    return pl.pallas_call(
        functools.partial(finish_kernel, n),
        out_shape=jax.ShapeDtypeStruct(spectra.shape, jnp.bfloat16),
        in_specs=[pl.BlockSpec(memory_space=pltpu.VMEM)] * 3,
        out_specs=pl.BlockSpec(memory_space=pltpu.HBM),
        scratch_shapes=[
            pltpu.VMEM((freq_count // 2, *spectra.shape[1:]), jnp.bfloat16),
            dma((major,)),
            dma((major,)),
        ],
        compiler_params=pltpu.CompilerParams(vmem_limit_bytes=32 * 1024 * 1024),
        name="finish_shapes",
    )(shapes, held, maps_pair)


def solution(mesh):
    in_specs = (P("freq", None, "pts", None), P("pts"))
    out_specs = P("freq", None, "pts", None)
    return jax.shard_map(
        functools.partial(local, mesh.shape["pts"]),
        mesh=mesh, in_specs=in_specs, out_specs=out_specs, check_vma=False,
    )
```

```python
import functools

import jax
import jax.numpy as jnp
from jax import lax
from jax.experimental import pallas as pl
from jax.experimental.pallas import tpu as pltpu
from jax.sharding import PartitionSpec as P

NS_STEPS = 10
MESH = pl.DeviceIdType.MESH


def places(shape):
    return (
        lax.broadcasted_iota(jnp.int32, shape, 0),
        lax.broadcasted_iota(jnp.int32, shape, 1),
    )


def pack(top):
    half, cols = top.shape
    row, lane = places(top.shape)
    left = lane < half
    upper = jnp.where(left, lane, lane - half) >= row
    rolled = pltpu.roll(top, half, 1)
    both = jnp.where(jnp.logical_xor(left, upper), rolled, top)
    quarter = half // 2
    return jnp.where(left[:quarter], both[:quarter], both[quarter:])


def unpack(packed):
    quarter, cols = packed.shape
    half = 2 * quarter
    left = places(packed.shape)[1] < half
    rolled = pltpu.roll(packed, half, 1)
    top = jnp.where(left, packed, rolled)
    bottom = jnp.where(left, rolled, packed)
    full = jnp.concatenate([top, bottom, top, bottom], 0)
    flipped = full.T
    row, lane = places(full.shape)
    row_left, lane_left = row < half, lane < half
    i = jnp.where(row_left, row, row - half)
    j = jnp.where(lane_left, lane, lane - half)
    real = jnp.where(j >= i, full, flipped)
    imag = jnp.where(j < i, full, jnp.where(j > i, -flipped, 0.0))
    imag = jnp.where(row_left, imag, -imag)
    return jnp.where(jnp.logical_xor(row_left, lane_left), imag, real)


def split(a):
    high = a.astype(jnp.bfloat16)
    low = (a - high.astype(jnp.float32)).astype(jnp.bfloat16)
    return high, low


def left_form(a):
    return jnp.concatenate(split(a), 1)


def product(left, right):
    wide = jnp.dot(left, right, preferred_element_type=jnp.float32)
    cols = wide.shape[1] // 2
    return wide[:, :cols] + wide[:, cols:]


def polar_map(crosses):
    order = crosses[0].shape[0]
    row, lane = places((order, order))
    eye = row == lane
    traces = [jnp.sum(jnp.where(eye, c, 0.0), keepdims=True) for c in crosses]
    grams = [c / t for c, t in zip(crosses, traces)]
    maps = [jnp.where(eye, 1.5 - 0.5 * g, -0.5 * g) for g in grams]
    for step in range(NS_STEPS):
        lefts = [left_form(g) for g in grams]
        rights = [jnp.concatenate([g, g], 0) for g in lefts]
        if step == 0:
            squares = [product(g, r) for g, r in zip(lefts, rights)]
        elif step < NS_STEPS - 1:
            both = [
                product(jnp.concatenate([g, left_form(q)], 0), r)
                for g, q, r in zip(lefts, maps, rights)
            ]
            squares = [x[:order] for x in both]
            maps = [1.5 * q - 0.5 * x[order:] for q, x in zip(maps, both)]
        else:
            maps = [1.5 * q - 0.5 * product(left_form(q), r) for q, r in zip(maps, rights)]
        if step < NS_STEPS - 1:
            halves = [1.5 * g - 0.5 * x for g, x in zip(grams, squares)]
            grams = [
                1.5 * t - 0.5 * product(left_form(t), r) for t, r in zip(halves, rights)
            ]
    return [q * lax.rsqrt(t) for q, t in zip(maps, traces)]


def apply(held, first, maps, out, place):
    group = len(maps)
    _, var_count, points, cols = held.shape
    maps = [m.astype(jnp.bfloat16) for m in maps]
    if group == 2:
        zero = jnp.zeros((cols, cols), jnp.bfloat16)
        right = jnp.concatenate(
            [
                jnp.concatenate([maps[0], zero], 1),
                jnp.concatenate([zero, maps[1]], 1),
            ],
            0,
        )
        for v in range(var_count):
            left = jnp.concatenate([held[first, v], held[first + 1, v]], 1)
            wide = jnp.dot(left, right, preferred_element_type=jnp.float32).astype(out.dtype)
            out[place, v] = wide[:, :cols]
            out[place + 1, v] = wide[:, cols:]
    else:
        for j in range(group):
            for v in range(var_count):
                out[place + j, v] = jnp.dot(
                    held[first + j, v], maps[j], preferred_element_type=jnp.float32
                ).astype(out.dtype)


def main_kernel(
    n, spectra, weights, out, held, maps_pair, row_weights, root, pair_out, pair_in, sums_out,
    sums_in, maps_out, maps_in, load_sem, weight_sem, pair_send, pair_recv, sum_send, sum_recv,
    map_send, map_recv, fwd_send, fwd_recv,
):
    major = n // 2
    me = lax.axis_index("pts")
    a, b = me // 2, lax.rem(me, 2)
    other = 1 - b
    partner = a * 2 + other
    _, var_count, points, cols = held.shape
    group = held.shape[0] // n
    half = cols // 2
    quarter = half // 2

    def ahead(d):
        return lax.rem(a + d, major)

    def behind(d):
        return lax.rem(a + major - d, major)

    def load(d, side):
        start = (ahead(d) * 2 + (b if side == 0 else other)) * group
        rows = pl.ds(start, group)
        return pltpu.make_async_copy(spectra.at[rows], held.at[rows], load_sem.at[side, d])

    def send(src, dst, send_sem, recv_sem, target):
        return pltpu.make_async_remote_copy(
            src_ref=src, dst_ref=dst, send_sem=send_sem, recv_sem=recv_sem,
            device_id={"pts": target}, device_id_type=MESH,
        )

    def pair_copy(d):
        return send(pair_out.at[d], pair_in.at[d], pair_send.at[d], pair_recv.at[d], partner)

    def sum_copy(d):
        return send(
            sums_out.at[d - 1], sums_in.at[d - 1], sum_send.at[d - 1], sum_recv.at[d - 1],
            ahead(d) * 2 + b,
        )

    def map_copy(d):
        return send(
            maps_out, maps_in.at[d - 1], map_send.at[d - 1], map_recv.at[d - 1], ahead(d) * 2 + b
        )

    via = major // 2

    def cross_copy(d):
        src = maps_in.at[d - 1] if d == via and d > 0 else maps_out
        target = partner if d == via else ahead(d) * 2 + other
        return send(src, maps_pair.at[d], fwd_send.at[d], fwd_recv.at[d], target)

    barrier = pltpu.get_barrier_semaphore()
    pl.semaphore_signal(barrier, inc=1, device_id={"pts": partner}, device_id_type=MESH)
    for d in range(1, major):
        pl.semaphore_signal(
            barrier, inc=1, device_id={"pts": ahead(d) * 2 + b}, device_id_type=MESH
        )
    for d in range(1, major):
        if d != via:
            pl.semaphore_signal(
                barrier, inc=1, device_id={"pts": ahead(d) * 2 + other}, device_id_type=MESH
            )
    weight_copy = pltpu.make_async_copy(weights, row_weights, weight_sem)
    weight_copy.start()
    for side in (1, 0):
        for d in range(1, major + 1):
            load(d % major, side).start()
    weight_copy.wait()
    root[...] = jnp.broadcast_to(jnp.sqrt(row_weights[...]), (cols, points)).T

    def fold(total):
        top, bottom = total[:half], pltpu.roll(total[half:], half, 1)
        lane = places(top.shape)[1]
        return pack(top + jnp.where(lane < half, bottom, -bottom))

    def packed_sums(first):
        sums = []
        for start in range(0, group, 2):
            count = min(2, group - start)
            rows = jnp.concatenate(
                [
                    (held[first + start + j].astype(jnp.float32) * root[...])
                    .astype(jnp.bfloat16)
                    .reshape(var_count * points, cols)
                    for j in range(count)
                ],
                1,
            )
            total = lax.dot_general(
                rows, rows, (((0,), (0,)), ((), ())), preferred_element_type=jnp.float32
            )
            for j in range(count):
                own_cols = slice(j * cols, (j + 1) * cols)
                sums.append(fold(total[own_cols, own_cols]))
        return sums

    def part(j):
        return pl.ds(j * quarter, quarter)

    def pair_sums(d):
        load(d, 1).wait()
        for j, packed in enumerate(packed_sums((ahead(d) * 2 + other) * group)):
            pair_out[d, part(j)] = packed

    early = min(2, major)

    @pl.loop(0, early)
    def _(i):
        pair_sums(lax.rem(i + 1, major))

    pl.semaphore_wait(barrier, major + max(major - 2, 0))
    for i in range(early):
        pair_copy((i + 1) % major).start()

    @pl.loop(early, major)
    def _(i):
        d = lax.rem(i + 1, major)
        pair_sums(d)
        pair_copy(d).start()

    @pl.loop(1, major)
    def _(d):
        load(d, 0).wait()
        sums = packed_sums((ahead(d) * 2 + b) * group)
        pair_copy(d).wait_recv()
        for j in range(group):
            sums_out[d - 1, part(j)] = sums[j] + pair_in[d, part(j)]
        sum_copy(d).start()

    load(0, 0).wait()
    own = packed_sums(me * group)
    pair_copy(0).wait_recv()
    for j in range(group):
        own[j] = own[j] + pair_in[0, part(j)]
    for d in range(1, major):
        sum_copy(d).wait_recv()
        for j in range(group):
            own[j] = own[j] + sums_in[d - 1, part(j)]

    maps = polar_map([unpack(o) for o in own])
    for j in range(group):
        maps_out[part(j)] = pack(maps[j][:half])
    def take(d):
        first = (behind(d) * 2 + b) * group
        apply(held, first, [unpack(maps_in[d - 1, part(j)]) for j in range(group)], out, first)

    if major > 1:
        map_copy(via).start()
    for d in range(1, major):
        if d != via:
            cross_copy(d).start()
            map_copy(d).start()
    cross_copy(0).start()
    apply(held, me * group, maps, out, me * group)
    if major > 1:
        map_copy(via).wait_recv()
        cross_copy(via).start()
        take(via)

    @pl.loop(0, major - 2)
    def _(i):
        d = lax.rem(via + i, major - 1) + 1
        map_copy(d).wait_recv()
        take(d)

    for d in range(major):
        cross_copy(d).wait_recv()

    for d in range(major):
        pair_copy(d).wait_send()
        cross_copy(d).wait_send()
        if d > 0:
            sum_copy(d).wait_send()
            map_copy(d).wait_send()


def finish_kernel(n, shapes, held, maps_pair, out, late, early_sem, late_sem):
    major = n // 2
    me = lax.axis_index("pts")
    a, b = me // 2, lax.rem(me, 2)
    group = held.shape[0] // n
    quarter = maps_pair.shape[1] // group

    def early_copy(d):
        rows = pl.ds((lax.rem(a + major - d, major) * 2 + b) * group, group)
        return pltpu.make_async_copy(shapes.at[rows], out.at[rows], early_sem.at[d])

    def late_first(d):
        return (lax.rem(a + major - d, major) * 2 + 1 - b) * group

    def late_copy(d):
        return pltpu.make_async_copy(
            late.at[pl.ds(d * group, group)],
            out.at[pl.ds(late_first(d), group)],
            late_sem.at[d],
        )

    for d in range(major):
        early_copy(d).start()

    @pl.loop(0, major)
    def _(d):
        maps = [unpack(maps_pair[d, pl.ds(j * quarter, quarter)]) for j in range(group)]
        apply(held, late_first(d), maps, late, d * group)
        late_copy(d).start()

    for d in range(major):
        early_copy(d).wait()
        late_copy(d).wait()


def local(n, spectra, weights):
    freq_count, var_count, points, cols = spectra.shape
    block = (freq_count // n * (cols // 4), cols)
    major = n // 2
    dma = pltpu.SemaphoreType.DMA
    shapes, held, maps_pair = pl.pallas_call(
        functools.partial(main_kernel, n),
        out_shape=[
            jax.ShapeDtypeStruct(spectra.shape, jnp.bfloat16),
            jax.ShapeDtypeStruct(spectra.shape, jnp.bfloat16),
            jax.ShapeDtypeStruct((major, *block), jnp.float32),
        ],
        in_specs=[pl.BlockSpec(memory_space=pltpu.HBM)] * 2,
        out_specs=[pl.BlockSpec(memory_space=pltpu.VMEM)] * 3,
        scratch_shapes=[
            pltpu.VMEM((1, points), jnp.float32),
            pltpu.VMEM((points, cols), jnp.float32),
            pltpu.VMEM((major, *block), jnp.float32),
            pltpu.VMEM((major, *block), jnp.float32),
            pltpu.VMEM((major - 1, *block), jnp.float32),
            pltpu.VMEM((major - 1, *block), jnp.float32),
            pltpu.VMEM(block, jnp.float32),
            pltpu.VMEM((major - 1, *block), jnp.float32),
            dma((2, major)),
            dma,
            dma((major,)),
            dma((major,)),
            dma((major - 1,)),
            dma((major - 1,)),
            dma((major - 1,)),
            dma((major - 1,)),
            dma((major,)),
            dma((major,)),
        ],
        compiler_params=pltpu.CompilerParams(
            collective_id=0, has_side_effects=True, vmem_limit_bytes=32 * 1024 * 1024
        ),
        name="polar_shapes",
    )(
        pltpu.with_memory_space_constraint(spectra, pltpu.HBM),
        pltpu.with_memory_space_constraint(weights.reshape(1, points), pltpu.HBM),
    )
    return pl.pallas_call(
        functools.partial(finish_kernel, n),
        out_shape=jax.ShapeDtypeStruct(spectra.shape, jnp.bfloat16),
        in_specs=[pl.BlockSpec(memory_space=pltpu.VMEM)] * 3,
        out_specs=pl.BlockSpec(memory_space=pltpu.HBM),
        scratch_shapes=[
            pltpu.VMEM((freq_count // 2, *spectra.shape[1:]), jnp.bfloat16),
            dma((major,)),
            dma((major,)),
        ],
        compiler_params=pltpu.CompilerParams(vmem_limit_bytes=32 * 1024 * 1024),
        name="finish_shapes",
    )(shapes, held, maps_pair)


def solution(mesh):
    in_specs = (P("freq", None, "pts", None), P("pts"))
    out_specs = P("freq", None, "pts", None)
    return jax.shard_map(
        functools.partial(local, mesh.shape["pts"]),
        mesh=mesh, in_specs=in_specs, out_specs=out_specs, check_vma=False,
    )
```

```python
import functools

import jax
import jax.numpy as jnp
from jax import lax
from jax.experimental import pallas as pl
from jax.experimental.pallas import tpu as pltpu
from jax.sharding import PartitionSpec as P

NS_STEPS = 10
MESH = pl.DeviceIdType.MESH


def places(shape):
    return (
        lax.broadcasted_iota(jnp.int32, shape, 0),
        lax.broadcasted_iota(jnp.int32, shape, 1),
    )


def pack(top):
    half, cols = top.shape
    row, lane = places(top.shape)
    left = lane < half
    upper = jnp.where(left, lane, lane - half) >= row
    rolled = pltpu.roll(top, half, 1)
    both = jnp.where(jnp.logical_xor(left, upper), rolled, top)
    quarter = half // 2
    return jnp.where(left[:quarter], both[:quarter], both[quarter:])


def unpack(packed):
    quarter, cols = packed.shape
    half = 2 * quarter
    left = places(packed.shape)[1] < half
    rolled = pltpu.roll(packed, half, 1)
    top = jnp.where(left, packed, rolled)
    bottom = jnp.where(left, rolled, packed)
    full = jnp.concatenate([top, bottom], 0)
    flipped = jnp.concatenate([full, full], 0).T[:half]
    row, lane = places(full.shape)
    left = lane < half
    j = jnp.where(left, lane, lane - half)
    real = jnp.where(j >= row, full, flipped)
    imag = jnp.where(j < row, full, jnp.where(j > row, -flipped, 0.0))
    return jnp.where(left, real, imag)


def complete(top):
    half = top.shape[0]
    rolled = pltpu.roll(top, half, 1)
    lane = places(top.shape)[1]
    return jnp.concatenate([top, jnp.where(lane < half, -rolled, rolled)], 0)


def split(a):
    high = a.astype(jnp.bfloat16)
    low = (a - high.astype(jnp.float32)).astype(jnp.bfloat16)
    return high, low


def left_form(a):
    return jnp.concatenate(split(a), 1)


def product(left, right):
    wide = jnp.dot(left, right, preferred_element_type=jnp.float32)
    cols = wide.shape[1] // 2
    return wide[:, :cols] + wide[:, cols:]


def polar_map(crosses):
    half = crosses[0].shape[0]
    row, lane = places(crosses[0].shape)
    eye = row == lane
    traces = [2.0 * jnp.sum(jnp.where(eye, c, 0.0), keepdims=True) for c in crosses]
    grams = [c / t for c, t in zip(crosses, traces)]
    maps = [jnp.where(eye, 1.5 - 0.5 * g, -0.5 * g) for g in grams]
    for step in range(NS_STEPS):
        fulls = [left_form(complete(g)) for g in grams]
        lefts = [g[:half] for g in fulls]
        rights = [jnp.concatenate([g, g], 0) for g in fulls]
        if step == 0:
            squares = [product(g, r) for g, r in zip(lefts, rights)]
        elif step < NS_STEPS - 1:
            both = [
                product(jnp.concatenate([g, left_form(q)], 0), r)
                for g, q, r in zip(lefts, maps, rights)
            ]
            squares = [x[:half] for x in both]
            maps = [1.5 * q - 0.5 * x[half:] for q, x in zip(maps, both)]
        else:
            maps = [1.5 * q - 0.5 * product(left_form(q), r) for q, r in zip(maps, rights)]
        if step < NS_STEPS - 1:
            halves = [1.5 * g - 0.5 * x for g, x in zip(grams, squares)]
            grams = [
                1.5 * t - 0.5 * product(left_form(t), r) for t, r in zip(halves, rights)
            ]
    return [q * lax.rsqrt(t) for q, t in zip(maps, traces)]


def apply(held, first, maps, out, place):
    group = len(maps)
    _, var_count, points, cols = held.shape
    maps = [complete(m).astype(jnp.bfloat16) for m in maps]
    if group == 2:
        zero = jnp.zeros((cols, cols), jnp.bfloat16)
        right = jnp.concatenate(
            [
                jnp.concatenate([maps[0], zero], 1),
                jnp.concatenate([zero, maps[1]], 1),
            ],
            0,
        )
        for v in range(var_count):
            left = jnp.concatenate([held[first, v], held[first + 1, v]], 1)
            wide = jnp.dot(left, right, preferred_element_type=jnp.float32).astype(out.dtype)
            out[place, v] = wide[:, :cols]
            out[place + 1, v] = wide[:, cols:]
    else:
        for j in range(group):
            for v in range(var_count):
                out[place + j, v] = jnp.dot(
                    held[first + j, v], maps[j], preferred_element_type=jnp.float32
                ).astype(out.dtype)


def main_kernel(
    n, spectra, weights, out, held, maps_pair, row_weights, root, pair_out, pair_in, sums_out,
    sums_in, maps_out, maps_in, load_sem, weight_sem, pair_send, pair_recv, sum_send, sum_recv,
    map_send, map_recv, fwd_send, fwd_recv,
):
    major = n // 2
    me = lax.axis_index("pts")
    a, b = me // 2, lax.rem(me, 2)
    other = 1 - b
    partner = a * 2 + other
    _, var_count, points, cols = held.shape
    group = held.shape[0] // n
    half = cols // 2
    quarter = half // 2

    def ahead(d):
        return lax.rem(a + d, major)

    def behind(d):
        return lax.rem(a + major - d, major)

    def load(d, side):
        start = (ahead(d) * 2 + (b if side == 0 else other)) * group
        rows = pl.ds(start, group)
        return pltpu.make_async_copy(spectra.at[rows], held.at[rows], load_sem.at[side, d])

    def send(src, dst, send_sem, recv_sem, target):
        return pltpu.make_async_remote_copy(
            src_ref=src, dst_ref=dst, send_sem=send_sem, recv_sem=recv_sem,
            device_id={"pts": target}, device_id_type=MESH,
        )

    def pair_copy(d):
        return send(pair_out.at[d], pair_in.at[d], pair_send.at[d], pair_recv.at[d], partner)

    def sum_copy(d):
        return send(
            sums_out.at[d - 1], sums_in.at[d - 1], sum_send.at[d - 1], sum_recv.at[d - 1],
            ahead(d) * 2 + b,
        )

    def map_copy(d):
        return send(
            maps_out, maps_in.at[d - 1], map_send.at[d - 1], map_recv.at[d - 1], ahead(d) * 2 + b
        )

    via = major // 2

    def cross_copy(d):
        src = maps_in.at[d - 1] if d == via and d > 0 else maps_out
        target = partner if d == via else ahead(d) * 2 + other
        return send(src, maps_pair.at[d], fwd_send.at[d], fwd_recv.at[d], target)

    barrier = pltpu.get_barrier_semaphore()
    pl.semaphore_signal(barrier, inc=1, device_id={"pts": partner}, device_id_type=MESH)
    for d in range(1, major):
        pl.semaphore_signal(
            barrier, inc=1, device_id={"pts": ahead(d) * 2 + b}, device_id_type=MESH
        )
    for d in range(1, major):
        if d != via:
            pl.semaphore_signal(
                barrier, inc=1, device_id={"pts": ahead(d) * 2 + other}, device_id_type=MESH
            )
    weight_copy = pltpu.make_async_copy(weights, row_weights, weight_sem)
    weight_copy.start()
    for side in (1, 0):
        for d in range(1, major + 1):
            load(d % major, side).start()
    weight_copy.wait()
    root[...] = jnp.broadcast_to(jnp.sqrt(row_weights[...]), (cols, points)).T

    def fold(total):
        top, bottom = total[:half], pltpu.roll(total[half:], half, 1)
        lane = places(top.shape)[1]
        return pack(top + jnp.where(lane < half, bottom, -bottom))

    def packed_sums(first):
        sums = []
        for start in range(0, group, 2):
            count = min(2, group - start)
            rows = jnp.concatenate(
                [
                    (held[first + start + j].astype(jnp.float32) * root[...])
                    .astype(jnp.bfloat16)
                    .reshape(var_count * points, cols)
                    for j in range(count)
                ],
                1,
            )
            total = lax.dot_general(
                rows, rows, (((0,), (0,)), ((), ())), preferred_element_type=jnp.float32
            )
            for j in range(count):
                own_cols = slice(j * cols, (j + 1) * cols)
                sums.append(fold(total[own_cols, own_cols]))
        return sums

    def part(j):
        return pl.ds(j * quarter, quarter)

    def pair_sums(d):
        load(d, 1).wait()
        for j, packed in enumerate(packed_sums((ahead(d) * 2 + other) * group)):
            pair_out[d, part(j)] = packed

    early = min(2, major)

    @pl.loop(0, early)
    def _(i):
        pair_sums(lax.rem(i + 1, major))

    pl.semaphore_wait(barrier, major + max(major - 2, 0))
    for i in range(early):
        pair_copy((i + 1) % major).start()

    @pl.loop(early, major)
    def _(i):
        d = lax.rem(i + 1, major)
        pair_sums(d)
        pair_copy(d).start()

    @pl.loop(1, major)
    def _(d):
        load(d, 0).wait()
        sums = packed_sums((ahead(d) * 2 + b) * group)
        pair_copy(d).wait_recv()
        for j in range(group):
            sums_out[d - 1, part(j)] = sums[j] + pair_in[d, part(j)]
        sum_copy(d).start()

    load(0, 0).wait()
    own = packed_sums(me * group)
    pair_copy(0).wait_recv()
    for j in range(group):
        own[j] = own[j] + pair_in[0, part(j)]
    for d in range(1, major):
        sum_copy(d).wait_recv()
        for j in range(group):
            own[j] = own[j] + sums_in[d - 1, part(j)]

    maps = polar_map([unpack(o) for o in own])
    for j in range(group):
        maps_out[part(j)] = pack(maps[j])
    def take(d):
        first = (behind(d) * 2 + b) * group
        apply(held, first, [unpack(maps_in[d - 1, part(j)]) for j in range(group)], out, first)

    if major > 1:
        map_copy(via).start()
    for d in range(1, major):
        if d != via:
            cross_copy(d).start()
            map_copy(d).start()
    cross_copy(0).start()
    apply(held, me * group, maps, out, me * group)
    if major > 1:
        map_copy(via).wait_recv()
        cross_copy(via).start()
        take(via)

    @pl.loop(0, major - 2)
    def _(i):
        d = lax.rem(via + i, major - 1) + 1
        map_copy(d).wait_recv()
        take(d)

    for d in range(major):
        cross_copy(d).wait_recv()

    for d in range(major):
        pair_copy(d).wait_send()
        cross_copy(d).wait_send()
        if d > 0:
            sum_copy(d).wait_send()
            map_copy(d).wait_send()


def finish_kernel(n, shapes, held, maps_pair, out, late, early_sem, late_sem):
    major = n // 2
    me = lax.axis_index("pts")
    a, b = me // 2, lax.rem(me, 2)
    group = held.shape[0] // n
    quarter = maps_pair.shape[1] // group

    def early_copy(d):
        rows = pl.ds((lax.rem(a + major - d, major) * 2 + b) * group, group)
        return pltpu.make_async_copy(shapes.at[rows], out.at[rows], early_sem.at[d])

    def late_first(d):
        return (lax.rem(a + major - d, major) * 2 + 1 - b) * group

    def late_copy(d):
        return pltpu.make_async_copy(
            late.at[pl.ds(d * group, group)],
            out.at[pl.ds(late_first(d), group)],
            late_sem.at[d],
        )

    for d in range(major):
        early_copy(d).start()

    @pl.loop(0, major)
    def _(d):
        maps = [unpack(maps_pair[d, pl.ds(j * quarter, quarter)]) for j in range(group)]
        apply(held, late_first(d), maps, late, d * group)
        late_copy(d).start()

    for d in range(major):
        early_copy(d).wait()
        late_copy(d).wait()


def local(n, spectra, weights):
    freq_count, var_count, points, cols = spectra.shape
    block = (freq_count // n * (cols // 4), cols)
    major = n // 2
    dma = pltpu.SemaphoreType.DMA
    shapes, held, maps_pair = pl.pallas_call(
        functools.partial(main_kernel, n),
        out_shape=[
            jax.ShapeDtypeStruct(spectra.shape, jnp.bfloat16),
            jax.ShapeDtypeStruct(spectra.shape, jnp.bfloat16),
            jax.ShapeDtypeStruct((major, *block), jnp.float32),
        ],
        in_specs=[pl.BlockSpec(memory_space=pltpu.HBM)] * 2,
        out_specs=[pl.BlockSpec(memory_space=pltpu.VMEM)] * 3,
        scratch_shapes=[
            pltpu.VMEM((1, points), jnp.float32),
            pltpu.VMEM((points, cols), jnp.float32),
            pltpu.VMEM((major, *block), jnp.float32),
            pltpu.VMEM((major, *block), jnp.float32),
            pltpu.VMEM((major - 1, *block), jnp.float32),
            pltpu.VMEM((major - 1, *block), jnp.float32),
            pltpu.VMEM(block, jnp.float32),
            pltpu.VMEM((major - 1, *block), jnp.float32),
            dma((2, major)),
            dma,
            dma((major,)),
            dma((major,)),
            dma((major - 1,)),
            dma((major - 1,)),
            dma((major - 1,)),
            dma((major - 1,)),
            dma((major,)),
            dma((major,)),
        ],
        compiler_params=pltpu.CompilerParams(
            collective_id=0, has_side_effects=True, vmem_limit_bytes=32 * 1024 * 1024
        ),
        name="polar_shapes",
    )(
        pltpu.with_memory_space_constraint(spectra, pltpu.HBM),
        pltpu.with_memory_space_constraint(weights.reshape(1, points), pltpu.HBM),
    )
    return pl.pallas_call(
        functools.partial(finish_kernel, n),
        out_shape=jax.ShapeDtypeStruct(spectra.shape, jnp.bfloat16),
        in_specs=[pl.BlockSpec(memory_space=pltpu.VMEM)] * 3,
        out_specs=pl.BlockSpec(memory_space=pltpu.HBM),
        scratch_shapes=[
            pltpu.VMEM((freq_count // 2, *spectra.shape[1:]), jnp.bfloat16),
            dma((major,)),
            dma((major,)),
        ],
        compiler_params=pltpu.CompilerParams(vmem_limit_bytes=32 * 1024 * 1024),
        name="finish_shapes",
    )(shapes, held, maps_pair)


def solution(mesh):
    in_specs = (P("freq", None, "pts", None), P("pts"))
    out_specs = P("freq", None, "pts", None)
    return jax.shard_map(
        functools.partial(local, mesh.shape["pts"]),
        mesh=mesh, in_specs=in_specs, out_specs=out_specs, check_vma=False,
    )
```

```python
import functools

import jax
import jax.numpy as jnp
from jax import lax
from jax.experimental import pallas as pl
from jax.experimental.pallas import tpu as pltpu
from jax.sharding import PartitionSpec as P

NS_STEPS = 10
MESH = pl.DeviceIdType.MESH


def places(shape):
    return (
        lax.broadcasted_iota(jnp.int32, shape, 0),
        lax.broadcasted_iota(jnp.int32, shape, 1),
    )


def pack(top):
    half, cols = top.shape
    row, lane = places(top.shape)
    left = lane < half
    upper = jnp.where(left, lane, lane - half) >= row
    rolled = pltpu.roll(top, half, 1)
    both = jnp.where(jnp.logical_xor(left, upper), rolled, top)
    quarter = half // 2
    return jnp.where(left[:quarter], both[:quarter], both[quarter:])


def unpack(packed):
    quarter, cols = packed.shape
    half = 2 * quarter
    left = places(packed.shape)[1] < half
    rolled = pltpu.roll(packed, half, 1)
    top = jnp.where(left, packed, rolled)
    bottom = jnp.where(left, rolled, packed)
    full = jnp.concatenate([top, bottom, top, bottom], 0)
    flipped = full.T
    row, lane = places(full.shape)
    row_left, lane_left = row < half, lane < half
    i = jnp.where(row_left, row, row - half)
    j = jnp.where(lane_left, lane, lane - half)
    real = jnp.where(j >= i, full, flipped)
    imag = jnp.where(j < i, full, jnp.where(j > i, -flipped, 0.0))
    imag = jnp.where(row_left, imag, -imag)
    return jnp.where(jnp.logical_xor(row_left, lane_left), imag, real)


def split(a):
    high = a.astype(jnp.bfloat16)
    low = (a - high.astype(jnp.float32)).astype(jnp.bfloat16)
    return high, low


def left_form(a):
    return jnp.concatenate(split(a), 1)


def product(left, right):
    wide = jnp.dot(left, right, preferred_element_type=jnp.float32)
    cols = wide.shape[1] // 2
    return wide[:, :cols] + wide[:, cols:]


def polar_map(crosses):
    order = crosses[0].shape[0]
    row, lane = places((order, order))
    eye = row == lane
    traces = [jnp.sum(jnp.where(eye, c, 0.0), keepdims=True) for c in crosses]
    grams = [c / t for c, t in zip(crosses, traces)]
    maps = [jnp.where(eye, 1.5 - 0.5 * g, -0.5 * g) for g in grams]
    for step in range(NS_STEPS):
        lefts = [left_form(g) for g in grams]
        rights = [jnp.concatenate([g, g], 0) for g in lefts]
        if step == 0:
            squares = [product(g, r) for g, r in zip(lefts, rights)]
        elif step < NS_STEPS - 1:
            both = [
                product(jnp.concatenate([g, left_form(q)], 0), r)
                for g, q, r in zip(lefts, maps, rights)
            ]
            squares = [x[:order] for x in both]
            maps = [1.5 * q - 0.5 * x[order:] for q, x in zip(maps, both)]
        else:
            maps = [1.5 * q - 0.5 * product(left_form(q), r) for q, r in zip(maps, rights)]
        if step < NS_STEPS - 1:
            halves = [1.5 * g - 0.5 * x for g, x in zip(grams, squares)]
            grams = [
                1.5 * t - 0.5 * product(left_form(t), r) for t, r in zip(halves, rights)
            ]
    return [q * lax.rsqrt(t) for q, t in zip(maps, traces)]


def apply(held, first, maps, out, place):
    group = len(maps)
    _, var_count, points, cols = held.shape
    maps = [m.astype(jnp.bfloat16) for m in maps]
    if group == 2:
        zero = jnp.zeros((cols, cols), jnp.bfloat16)
        right = jnp.concatenate(
            [
                jnp.concatenate([maps[0], zero], 1),
                jnp.concatenate([zero, maps[1]], 1),
            ],
            0,
        )
        for v in range(var_count):
            left = jnp.concatenate([held[first, v], held[first + 1, v]], 1)
            wide = jnp.dot(left, right, preferred_element_type=jnp.float32).astype(out.dtype)
            out[place, v] = wide[:, :cols]
            out[place + 1, v] = wide[:, cols:]
    else:
        for j in range(group):
            for v in range(var_count):
                out[place + j, v] = jnp.dot(
                    held[first + j, v], maps[j], preferred_element_type=jnp.float32
                ).astype(out.dtype)


def offset(n, i):
    return lax.rem(n // 2 - 1 + i, n - 1) + 1


def main_kernel(
    n, late, spectra, weights, out, held, maps_in, row_weights, root, sums_out, sums_in, maps_out,
    load_sem, weight_sem, sum_send, sum_recv, map_send, map_recv,
):
    me = lax.axis_index("pts")
    _, var_count, points, cols = held.shape
    group = held.shape[0] // n
    half = cols // 2
    quarter = half // 2

    def peer(i):
        return lax.rem(me + offset(n, i), n)

    def load(i):
        owner = me if isinstance(i, int) and i == n - 1 else peer(i)
        rows = pl.ds(owner * group, group)
        return pltpu.make_async_copy(spectra.at[rows], held.at[rows], load_sem.at[i])

    def sum_copy(i):
        return pltpu.make_async_remote_copy(
            src_ref=sums_out.at[i], dst_ref=sums_in.at[i], send_sem=sum_send.at[i],
            recv_sem=sum_recv.at[i], device_id={"pts": peer(i)}, device_id_type=MESH,
        )

    def map_copy(i):
        return pltpu.make_async_remote_copy(
            src_ref=maps_out, dst_ref=maps_in.at[i], send_sem=map_send.at[i],
            recv_sem=map_recv.at[i], device_id={"pts": peer(i)}, device_id_type=MESH,
        )

    barrier = pltpu.get_barrier_semaphore()
    for i in range(n - 1):
        pl.semaphore_signal(barrier, inc=1, device_id={"pts": peer(i)}, device_id_type=MESH)
    weight_copy = pltpu.make_async_copy(weights, row_weights, weight_sem)
    weight_copy.start()
    for i in range(n):
        load(i).start()
    weight_copy.wait()
    root[...] = jnp.broadcast_to(jnp.sqrt(row_weights[...]), (cols, points)).T

    def fold(total):
        top, bottom = total[:half], pltpu.roll(total[half:], half, 1)
        lane = places(top.shape)[1]
        return pack(top + jnp.where(lane < half, bottom, -bottom))

    def packed_sums(first):
        sums = []
        for start in range(0, group, 2):
            count = min(2, group - start)
            rows = jnp.concatenate(
                [
                    (held[first + start + j].astype(jnp.float32) * root[...])
                    .astype(jnp.bfloat16)
                    .reshape(var_count * points, cols)
                    for j in range(count)
                ],
                1,
            )
            total = lax.dot_general(
                rows, rows, (((0,), (0,)), ((), ())), preferred_element_type=jnp.float32
            )
            for j in range(count):
                own_cols = slice(j * cols, (j + 1) * cols)
                sums.append(fold(total[own_cols, own_cols]))
        return sums

    def part(j):
        return pl.ds(j * quarter, quarter)

    def peer_sums(i):
        load(i).wait()
        for j, packed in enumerate(packed_sums(peer(i) * group)):
            sums_out[i, part(j)] = packed

    early = min(2, n - 1)

    @pl.loop(0, early)
    def _(i):
        peer_sums(i)

    pl.semaphore_wait(barrier, n - 1)
    for i in range(early):
        sum_copy(i).start()

    @pl.loop(early, n - 1)
    def _(i):
        peer_sums(i)
        sum_copy(i).start()

    load(n - 1).wait()
    own = packed_sums(me * group)
    for i in range(n - 1):
        sum_copy(i).wait_recv()
        for j in range(group):
            own[j] = own[j] + sums_in[i, part(j)]

    maps = polar_map([unpack(o) for o in own])
    for j in range(group):
        maps_out[part(j)] = pack(maps[j][:half])
    for i in range(n - 1):
        map_copy(i).start()
    apply(held, me * group, maps, out, me * group)

    @pl.loop(0, n - 1 - late)
    def _(i):
        map_copy(i).wait_recv()
        first = lax.rem(me + n - offset(n, i), n) * group
        apply(held, first, [unpack(maps_in[i, part(j)]) for j in range(group)], out, first)

    for i in range(n - 1 - late, n - 1):
        map_copy(i).wait_recv()
    for i in range(n - 1):
        sum_copy(i).wait_send()
        map_copy(i).wait_send()


def finish_kernel(n, late, shapes, held, maps_in, out, late_shapes, early_sem, late_sem):
    me = lax.axis_index("pts")
    group = held.shape[0] // n
    quarter = maps_in.shape[1] // group
    early = n - 1 - late

    def first(i):
        return lax.rem(me + n - offset(n, i), n) * group

    def early_copy(i):
        rows = pl.ds(me * group if i == early else first(i), group)
        return pltpu.make_async_copy(shapes.at[rows], out.at[rows], early_sem.at[i])

    def late_copy(i):
        return pltpu.make_async_copy(
            late_shapes.at[pl.ds(i * group, group)],
            out.at[pl.ds(first(early + i), group)],
            late_sem.at[i],
        )

    for i in range(early + 1):
        early_copy(i).start()

    @pl.loop(0, late)
    def _(i):
        slot = early + i
        maps = [unpack(maps_in[slot, pl.ds(j * quarter, quarter)]) for j in range(group)]
        apply(held, first(slot), maps, late_shapes, i * group)
        late_copy(i).start()

    for i in range(early + 1):
        early_copy(i).wait()
    for i in range(late):
        late_copy(i).wait()


def local(n, spectra, weights):
    freq_count, var_count, points, cols = spectra.shape
    group = freq_count // n
    slots = (n - 1, group * (cols // 4), cols)
    late = max(1, n // 2 - 1)
    dma = pltpu.SemaphoreType.DMA
    params = dict(vmem_limit_bytes=32 * 1024 * 1024)
    shapes, held, maps_in = pl.pallas_call(
        functools.partial(main_kernel, n, late),
        out_shape=[
            jax.ShapeDtypeStruct(spectra.shape, jnp.bfloat16),
            jax.ShapeDtypeStruct(spectra.shape, jnp.bfloat16),
            jax.ShapeDtypeStruct(slots, jnp.float32),
        ],
        in_specs=[pl.BlockSpec(memory_space=pltpu.HBM)] * 2,
        out_specs=[pl.BlockSpec(memory_space=pltpu.VMEM)] * 3,
        scratch_shapes=[
            pltpu.VMEM((1, points), jnp.float32),
            pltpu.VMEM((points, cols), jnp.float32),
            pltpu.VMEM(slots, jnp.float32),
            pltpu.VMEM(slots, jnp.float32),
            pltpu.VMEM(slots[1:], jnp.float32),
            dma((n,)),
            dma,
            dma((n - 1,)),
            dma((n - 1,)),
            dma((n - 1,)),
            dma((n - 1,)),
        ],
        compiler_params=pltpu.CompilerParams(collective_id=0, has_side_effects=True, **params),
        name="polar_shapes",
    )(
        pltpu.with_memory_space_constraint(spectra, pltpu.HBM),
        pltpu.with_memory_space_constraint(weights.reshape(1, points), pltpu.HBM),
    )
    return pl.pallas_call(
        functools.partial(finish_kernel, n, late),
        out_shape=jax.ShapeDtypeStruct(spectra.shape, jnp.bfloat16),
        in_specs=[pl.BlockSpec(memory_space=pltpu.VMEM)] * 3,
        out_specs=pl.BlockSpec(memory_space=pltpu.HBM),
        scratch_shapes=[
            pltpu.VMEM((late * group, *spectra.shape[1:]), jnp.bfloat16),
            dma((n - late,)),
            dma((late,)),
        ],
        compiler_params=pltpu.CompilerParams(**params),
        name="finish_shapes",
    )(shapes, held, maps_in)


def solution(mesh):
    in_specs = (P("freq", None, "pts", None), P("pts"))
    out_specs = P("freq", None, "pts", None)
    return jax.shard_map(
        functools.partial(local, mesh.shape["pts"]),
        mesh=mesh, in_specs=in_specs, out_specs=out_specs, check_vma=False,
    )
```

```python
import functools

import jax
import jax.numpy as jnp
from jax import lax
from jax.experimental import pallas as pl
from jax.experimental.pallas import tpu as pltpu
from jax.sharding import PartitionSpec as P

NS_STEPS = 10
MESH = pl.DeviceIdType.MESH


def places(shape):
    return (
        lax.broadcasted_iota(jnp.int32, shape, 0),
        lax.broadcasted_iota(jnp.int32, shape, 1),
    )


def pack(top):
    half, cols = top.shape
    row, lane = places(top.shape)
    left = lane < half
    upper = jnp.where(left, lane, lane - half) >= row
    rolled = pltpu.roll(top, half, 1)
    both = jnp.where(jnp.logical_xor(left, upper), rolled, top)
    quarter = half // 2
    return jnp.where(left[:quarter], both[:quarter], both[quarter:])


def unpack(packed):
    quarter, cols = packed.shape
    half = 2 * quarter
    left = places(packed.shape)[1] < half
    rolled = pltpu.roll(packed, half, 1)
    top = jnp.where(left, packed, rolled)
    bottom = jnp.where(left, rolled, packed)
    full = jnp.concatenate([top, bottom, top, bottom], 0)
    flipped = full.T
    row, lane = places(full.shape)
    row_left, lane_left = row < half, lane < half
    i = jnp.where(row_left, row, row - half)
    j = jnp.where(lane_left, lane, lane - half)
    real = jnp.where(j >= i, full, flipped)
    imag = jnp.where(j < i, full, jnp.where(j > i, -flipped, 0.0))
    imag = jnp.where(row_left, imag, -imag)
    return jnp.where(jnp.logical_xor(row_left, lane_left), imag, real)


def split(a):
    high = a.astype(jnp.bfloat16)
    low = (a - high.astype(jnp.float32)).astype(jnp.bfloat16)
    return high, low


def left_form(a):
    return jnp.concatenate(split(a), 1)


def product(left, right):
    wide = jnp.dot(left, right, preferred_element_type=jnp.float32)
    cols = wide.shape[1] // 2
    return wide[:, :cols] + wide[:, cols:]


def polar_map(crosses):
    order = crosses[0].shape[0]
    row, lane = places((order, order))
    eye = row == lane
    traces = [jnp.sum(jnp.where(eye, c, 0.0), keepdims=True) for c in crosses]
    grams = [c / t for c, t in zip(crosses, traces)]
    maps = [jnp.where(eye, 1.5 - 0.5 * g, -0.5 * g) for g in grams]
    for step in range(NS_STEPS):
        lefts = [left_form(g) for g in grams]
        rights = [jnp.concatenate([g, g], 0) for g in lefts]
        if step == 0:
            squares = [product(g, r) for g, r in zip(lefts, rights)]
        elif step < NS_STEPS - 1:
            both = [
                product(jnp.concatenate([g, left_form(q)], 0), r)
                for g, q, r in zip(lefts, maps, rights)
            ]
            squares = [x[:order] for x in both]
            maps = [1.5 * q - 0.5 * x[order:] for q, x in zip(maps, both)]
        else:
            maps = [1.5 * q - 0.5 * product(left_form(q), r) for q, r in zip(maps, rights)]
        if step < NS_STEPS - 1:
            halves = [1.5 * g - 0.5 * x for g, x in zip(grams, squares)]
            grams = [
                1.5 * t - 0.5 * product(left_form(t), r) for t, r in zip(halves, rights)
            ]
    return [q * lax.rsqrt(t) for q, t in zip(maps, traces)]


def apply(held, first, maps, out, place):
    group = len(maps)
    _, var_count, points, cols = held.shape
    maps = [m.astype(jnp.bfloat16) for m in maps]
    if group == 2:
        zero = jnp.zeros((cols, cols), jnp.bfloat16)
        right = jnp.concatenate(
            [
                jnp.concatenate([maps[0], zero], 1),
                jnp.concatenate([zero, maps[1]], 1),
            ],
            0,
        )
        for v in range(var_count):
            left = jnp.concatenate([held[first, v], held[first + 1, v]], 1)
            wide = jnp.dot(left, right, preferred_element_type=jnp.float32).astype(out.dtype)
            out[place, v] = wide[:, :cols]
            out[place + 1, v] = wide[:, cols:]
    else:
        for j in range(group):
            for v in range(var_count):
                out[place + j, v] = jnp.dot(
                    held[first + j, v], maps[j], preferred_element_type=jnp.float32
                ).astype(out.dtype)


def main_kernel(
    n, spectra, weights, out, held, maps_pair, row_weights, root, pair_out, pair_in, sums_out,
    sums_in, maps_out, maps_in, load_sem, weight_sem, pair_send, pair_recv, sum_send, sum_recv,
    map_send, map_recv, cross_send, cross_recv,
):
    major = n // 2
    me = lax.axis_index("pts")
    a, b = me // 2, lax.rem(me, 2)
    other = 1 - b
    partner = a * 2 + other
    _, var_count, points, cols = held.shape
    group = held.shape[0] // n
    half = cols // 2
    quarter = half // 2

    def ahead(d):
        return lax.rem(a + d, major)

    def behind(d):
        return lax.rem(a + major - d, major)

    def load(d, side):
        start = (ahead(d) * 2 + (b if side == 0 else other)) * group
        rows = pl.ds(start, group)
        return pltpu.make_async_copy(spectra.at[rows], held.at[rows], load_sem.at[side, d])

    def send(src, dst, send_sem, recv_sem, target):
        return pltpu.make_async_remote_copy(
            src_ref=src, dst_ref=dst, send_sem=send_sem, recv_sem=recv_sem,
            device_id={"pts": target}, device_id_type=MESH,
        )

    def pair_copy(d):
        return send(pair_out.at[d], pair_in.at[d], pair_send.at[d], pair_recv.at[d], partner)

    def sum_copy(d):
        return send(
            sums_out.at[d - 1], sums_in.at[d - 1], sum_send.at[d - 1], sum_recv.at[d - 1],
            ahead(d) * 2 + b,
        )

    def map_copy(d):
        return send(
            maps_out, maps_in.at[d - 1], map_send.at[d - 1], map_recv.at[d - 1], ahead(d) * 2 + b
        )

    def cross_copy(d):
        src = maps_in.at[d - 1] if d > 0 else maps_out
        return send(src, maps_pair.at[d], cross_send.at[d], cross_recv.at[d], partner)

    barrier = pltpu.get_barrier_semaphore()
    pl.semaphore_signal(barrier, inc=1, device_id={"pts": partner}, device_id_type=MESH)
    for d in range(1, major):
        pl.semaphore_signal(
            barrier, inc=1, device_id={"pts": ahead(d) * 2 + b}, device_id_type=MESH
        )
    weight_copy = pltpu.make_async_copy(weights, row_weights, weight_sem)
    weight_copy.start()
    for side in (1, 0):
        for d in range(1, major + 1):
            load(d % major, side).start()
    weight_copy.wait()
    root[...] = jnp.broadcast_to(jnp.sqrt(row_weights[...]), (cols, points)).T

    def fold(total):
        top, bottom = total[:half], pltpu.roll(total[half:], half, 1)
        lane = places(top.shape)[1]
        return pack(top + jnp.where(lane < half, bottom, -bottom))

    def packed_sums(first):
        sums = []
        for start in range(0, group, 2):
            count = min(2, group - start)
            rows = jnp.concatenate(
                [
                    (held[first + start + j].astype(jnp.float32) * root[...])
                    .astype(jnp.bfloat16)
                    .reshape(var_count * points, cols)
                    for j in range(count)
                ],
                1,
            )
            total = lax.dot_general(
                rows, rows, (((0,), (0,)), ((), ())), preferred_element_type=jnp.float32
            )
            for j in range(count):
                own_cols = slice(j * cols, (j + 1) * cols)
                sums.append(fold(total[own_cols, own_cols]))
        return sums

    def part(j):
        return pl.ds(j * quarter, quarter)

    def pair_sums(d):
        load(d, 1).wait()
        for j, packed in enumerate(packed_sums((ahead(d) * 2 + other) * group)):
            pair_out[d, part(j)] = packed

    early = min(2, major)

    @pl.loop(0, early)
    def _(i):
        pair_sums(lax.rem(i + 1, major))

    pl.semaphore_wait(barrier, major)
    for i in range(early):
        pair_copy((i + 1) % major).start()

    @pl.loop(early, major)
    def _(i):
        d = lax.rem(i + 1, major)
        pair_sums(d)
        pair_copy(d).start()

    @pl.loop(1, major)
    def _(d):
        load(d, 0).wait()
        sums = packed_sums((ahead(d) * 2 + b) * group)
        pair_copy(d).wait_recv()
        for j in range(group):
            sums_out[d - 1, part(j)] = sums[j] + pair_in[d, part(j)]
        sum_copy(d).start()

    load(0, 0).wait()
    own = packed_sums(me * group)
    pair_copy(0).wait_recv()
    for j in range(group):
        own[j] = own[j] + pair_in[0, part(j)]
    for d in range(1, major):
        sum_copy(d).wait_recv()
        for j in range(group):
            own[j] = own[j] + sums_in[d - 1, part(j)]

    maps = polar_map([unpack(o) for o in own])
    for j in range(group):
        maps_out[part(j)] = pack(maps[j][:half])
    order = sorted(range(1, major), key=lambda d: abs(d - major // 2))
    for d in order:
        map_copy(d).start()
    cross_copy(0).start()
    apply(held, me * group, maps, out, me * group)
    for d in order:
        map_copy(d).wait_recv()
        cross_copy(d).start()

    @pl.loop(1, major)
    def _(d):
        first = (behind(d) * 2 + b) * group
        apply(held, first, [unpack(maps_in[d - 1, part(j)]) for j in range(group)], out, first)

    cross_copy(0).wait_recv()
    first = partner * group
    apply(held, first, [unpack(maps_pair[0, part(j)]) for j in range(group)], out, first)
    for d in order:
        cross_copy(d).wait_recv()

    for d in range(major):
        pair_copy(d).wait_send()
        cross_copy(d).wait_send()
        if d > 0:
            sum_copy(d).wait_send()
            map_copy(d).wait_send()


def finish_kernel(n, shapes, held, maps_pair, out, late, early_sem, late_sem):
    major = n // 2
    me = lax.axis_index("pts")
    a, b = me // 2, lax.rem(me, 2)
    group = held.shape[0] // n
    quarter = maps_pair.shape[1] // group

    def early_copy(d):
        rows = pl.ds((lax.rem(a + major - d, major) * 2 + b) * group, group)
        return pltpu.make_async_copy(shapes.at[rows], out.at[rows], early_sem.at[d])

    def late_first(d):
        return (lax.rem(a + major - d, major) * 2 + 1 - b) * group

    def late_copy(d):
        return pltpu.make_async_copy(
            late.at[pl.ds((d - 1) * group, group)],
            out.at[pl.ds(late_first(d), group)],
            late_sem.at[d],
        )

    pair_rows = pl.ds(late_first(0), group)
    pair_copy = pltpu.make_async_copy(shapes.at[pair_rows], out.at[pair_rows], late_sem.at[0])
    for d in range(major):
        early_copy(d).start()
    pair_copy.start()

    @pl.loop(1, major)
    def _(d):
        maps = [unpack(maps_pair[d, pl.ds(j * quarter, quarter)]) for j in range(group)]
        apply(held, late_first(d), maps, late, (d - 1) * group)
        late_copy(d).start()

    for d in range(major):
        early_copy(d).wait()
    pair_copy.wait()
    for d in range(1, major):
        late_copy(d).wait()


def local(n, spectra, weights):
    freq_count, var_count, points, cols = spectra.shape
    block = (freq_count // n * (cols // 4), cols)
    major = n // 2
    dma = pltpu.SemaphoreType.DMA
    shapes, held, maps_pair = pl.pallas_call(
        functools.partial(main_kernel, n),
        out_shape=[
            jax.ShapeDtypeStruct(spectra.shape, jnp.bfloat16),
            jax.ShapeDtypeStruct(spectra.shape, jnp.bfloat16),
            jax.ShapeDtypeStruct((major, *block), jnp.float32),
        ],
        in_specs=[pl.BlockSpec(memory_space=pltpu.HBM)] * 2,
        out_specs=[pl.BlockSpec(memory_space=pltpu.VMEM)] * 3,
        scratch_shapes=[
            pltpu.VMEM((1, points), jnp.float32),
            pltpu.VMEM((points, cols), jnp.float32),
            pltpu.VMEM((major, *block), jnp.float32),
            pltpu.VMEM((major, *block), jnp.float32),
            pltpu.VMEM((major - 1, *block), jnp.float32),
            pltpu.VMEM((major - 1, *block), jnp.float32),
            pltpu.VMEM(block, jnp.float32),
            pltpu.VMEM((major - 1, *block), jnp.float32),
            dma((2, major)),
            dma,
            dma((major,)),
            dma((major,)),
            dma((major - 1,)),
            dma((major - 1,)),
            dma((major - 1,)),
            dma((major - 1,)),
            dma((major,)),
            dma((major,)),
        ],
        compiler_params=pltpu.CompilerParams(
            collective_id=0, has_side_effects=True, vmem_limit_bytes=32 * 1024 * 1024
        ),
        name="polar_shapes",
    )(
        pltpu.with_memory_space_constraint(spectra, pltpu.HBM),
        pltpu.with_memory_space_constraint(weights.reshape(1, points), pltpu.HBM),
    )
    return pl.pallas_call(
        functools.partial(finish_kernel, n),
        out_shape=jax.ShapeDtypeStruct(spectra.shape, jnp.bfloat16),
        in_specs=[pl.BlockSpec(memory_space=pltpu.VMEM)] * 3,
        out_specs=pl.BlockSpec(memory_space=pltpu.HBM),
        scratch_shapes=[
            pltpu.VMEM((max(1, freq_count // 2 - freq_count // n), *spectra.shape[1:]), jnp.bfloat16),
            dma((major,)),
            dma((major,)),
        ],
        compiler_params=pltpu.CompilerParams(vmem_limit_bytes=32 * 1024 * 1024),
        name="finish_shapes",
    )(shapes, held, maps_pair)


def solution(mesh):
    in_specs = (P("freq", None, "pts", None), P("pts"))
    out_specs = P("freq", None, "pts", None)
    return jax.shard_map(
        functools.partial(local, mesh.shape["pts"]),
        mesh=mesh, in_specs=in_specs, out_specs=out_specs, check_vma=False,
    )
```

```python
import functools

import jax
import jax.numpy as jnp
from jax import lax
from jax.experimental import pallas as pl
from jax.experimental.pallas import tpu as pltpu
from jax.sharding import PartitionSpec as P

NS_STEPS = 10
MESH = pl.DeviceIdType.MESH


def places(shape):
    return (
        lax.broadcasted_iota(jnp.int32, shape, 0),
        lax.broadcasted_iota(jnp.int32, shape, 1),
    )


def pack(top):
    half, cols = top.shape
    row, lane = places(top.shape)
    left = lane < half
    upper = jnp.where(left, lane, lane - half) >= row
    rolled = pltpu.roll(top, half, 1)
    both = jnp.where(jnp.logical_xor(left, upper), rolled, top)
    quarter = half // 2
    return jnp.where(left[:quarter], both[:quarter], both[quarter:])


def unpack(packed):
    quarter, cols = packed.shape
    half = 2 * quarter
    left = places(packed.shape)[1] < half
    rolled = pltpu.roll(packed, half, 1)
    top = jnp.where(left, packed, rolled)
    bottom = jnp.where(left, rolled, packed)
    full = jnp.concatenate([top, bottom, top, bottom], 0)
    flipped = full.T
    row, lane = places(full.shape)
    row_left, lane_left = row < half, lane < half
    i = jnp.where(row_left, row, row - half)
    j = jnp.where(lane_left, lane, lane - half)
    real = jnp.where(j >= i, full, flipped)
    imag = jnp.where(j < i, full, jnp.where(j > i, -flipped, 0.0))
    imag = jnp.where(row_left, imag, -imag)
    return jnp.where(jnp.logical_xor(row_left, lane_left), imag, real)


def split(a):
    high = a.astype(jnp.bfloat16)
    low = (a - high.astype(jnp.float32)).astype(jnp.bfloat16)
    return high, low


def left_form(a):
    return jnp.concatenate(split(a), 1)


def product(left, right):
    wide = jnp.dot(left, right, preferred_element_type=jnp.float32)
    cols = wide.shape[1] // 2
    return wide[:, :cols] + wide[:, cols:]


def polar_map(crosses):
    order = crosses[0].shape[0]
    row, lane = places((order, order))
    eye = row == lane
    traces = [jnp.sum(jnp.where(eye, c, 0.0), keepdims=True) for c in crosses]
    grams = [c / t for c, t in zip(crosses, traces)]
    maps = [jnp.where(eye, 1.5 - 0.5 * g, -0.5 * g) for g in grams]
    for step in range(NS_STEPS):
        lefts = [left_form(g) for g in grams]
        rights = [jnp.concatenate([g, g], 0) for g in lefts]
        if step == 0:
            squares = [product(g, r) for g, r in zip(lefts, rights)]
        elif step < NS_STEPS - 1:
            both = [
                product(jnp.concatenate([g, left_form(q)], 0), r)
                for g, q, r in zip(lefts, maps, rights)
            ]
            squares = [x[:order] for x in both]
            maps = [1.5 * q - 0.5 * x[order:] for q, x in zip(maps, both)]
        else:
            maps = [1.5 * q - 0.5 * product(left_form(q), r) for q, r in zip(maps, rights)]
        if step < NS_STEPS - 1:
            halves = [1.5 * g - 0.5 * x for g, x in zip(grams, squares)]
            grams = [
                1.5 * t - 0.5 * product(left_form(t), r) for t, r in zip(halves, rights)
            ]
    return [q * lax.rsqrt(t) for q, t in zip(maps, traces)]


def apply(held, first, maps, out, place):
    group = len(maps)
    _, var_count, points, cols = held.shape
    maps = [m.astype(jnp.bfloat16) for m in maps]
    if group == 2:
        zero = jnp.zeros((cols, cols), jnp.bfloat16)
        right = jnp.concatenate(
            [
                jnp.concatenate([maps[0], zero], 1),
                jnp.concatenate([zero, maps[1]], 1),
            ],
            0,
        )
        for v in range(var_count):
            left = jnp.concatenate([held[first, v], held[first + 1, v]], 1)
            wide = jnp.dot(left, right, preferred_element_type=jnp.float32).astype(out.dtype)
            out[place, v] = wide[:, :cols]
            out[place + 1, v] = wide[:, cols:]
    else:
        for j in range(group):
            for v in range(var_count):
                out[place + j, v] = jnp.dot(
                    held[first + j, v], maps[j], preferred_element_type=jnp.float32
                ).astype(out.dtype)


def main_kernel(
    n, spectra, weights, out, held, maps_pair, row_weights, root, pair_out, pair_in, sums_out,
    sums_in, maps_out, maps_in, load_sem, weight_sem, pair_send, pair_recv, sum_send, sum_recv,
    map_send, map_recv, cross_send, cross_recv,
):
    major = n // 2
    me = lax.axis_index("pts")
    a, b = me // 2, lax.rem(me, 2)
    other = 1 - b
    partner = a * 2 + other
    _, var_count, points, cols = held.shape
    group = held.shape[0] // n
    half = cols // 2
    quarter = half // 2

    def ahead(d):
        return lax.rem(a + d, major)

    def behind(d):
        return lax.rem(a + major - d, major)

    def load(d, side):
        start = (ahead(d) * 2 + (b if side == 0 else other)) * group
        rows = pl.ds(start, group)
        return pltpu.make_async_copy(spectra.at[rows], held.at[rows], load_sem.at[side, d])

    def send(src, dst, send_sem, recv_sem, target):
        return pltpu.make_async_remote_copy(
            src_ref=src, dst_ref=dst, send_sem=send_sem, recv_sem=recv_sem,
            device_id={"pts": target}, device_id_type=MESH,
        )

    def pair_copy(d):
        return send(pair_out.at[d], pair_in.at[d], pair_send.at[d], pair_recv.at[d], partner)

    def sum_copy(d):
        return send(
            sums_out.at[d - 1], sums_in.at[d - 1], sum_send.at[d - 1], sum_recv.at[d - 1],
            ahead(d) * 2 + b,
        )

    def map_copy(d):
        return send(
            maps_out, maps_in.at[d - 1], map_send.at[d - 1], map_recv.at[d - 1], ahead(d) * 2 + b
        )

    via = major // 2

    def cross_copy(d):
        src = maps_in.at[d - 1] if d == via and d > 0 else maps_out
        target = partner if d == via else ahead(d) * 2 + other
        return send(src, maps_pair.at[d], cross_send.at[d], cross_recv.at[d], target)

    barrier = pltpu.get_barrier_semaphore()
    pl.semaphore_signal(barrier, inc=1, device_id={"pts": partner}, device_id_type=MESH)
    for d in range(1, major):
        pl.semaphore_signal(
            barrier, inc=1, device_id={"pts": ahead(d) * 2 + b}, device_id_type=MESH
        )
    for d in range(1, major):
        if d != via:
            pl.semaphore_signal(
                barrier, inc=1, device_id={"pts": ahead(d) * 2 + other}, device_id_type=MESH
            )
    weight_copy = pltpu.make_async_copy(weights, row_weights, weight_sem)
    weight_copy.start()
    for side in (1, 0):
        for d in range(1, major + 1):
            load(d % major, side).start()
    weight_copy.wait()
    root[...] = jnp.broadcast_to(jnp.sqrt(row_weights[...]), (cols, points)).T

    def fold(total):
        top, bottom = total[:half], pltpu.roll(total[half:], half, 1)
        lane = places(top.shape)[1]
        return pack(top + jnp.where(lane < half, bottom, -bottom))

    def packed_sums(first):
        sums = []
        for start in range(0, group, 2):
            count = min(2, group - start)
            rows = jnp.concatenate(
                [
                    (held[first + start + j].astype(jnp.float32) * root[...])
                    .astype(jnp.bfloat16)
                    .reshape(var_count * points, cols)
                    for j in range(count)
                ],
                1,
            )
            total = lax.dot_general(
                rows, rows, (((0,), (0,)), ((), ())), preferred_element_type=jnp.float32
            )
            for j in range(count):
                own_cols = slice(j * cols, (j + 1) * cols)
                sums.append(fold(total[own_cols, own_cols]))
        return sums

    def part(j):
        return pl.ds(j * quarter, quarter)

    def pair_sums(d):
        load(d, 1).wait()
        for j, packed in enumerate(packed_sums((ahead(d) * 2 + other) * group)):
            pair_out[d, part(j)] = packed

    early = min(2, major)

    @pl.loop(0, early)
    def _(i):
        pair_sums(lax.rem(i + 1, major))

    pl.semaphore_wait(barrier, major + max(major - 2, 0))
    for i in range(early):
        pair_copy((i + 1) % major).start()

    @pl.loop(early, major)
    def _(i):
        d = lax.rem(i + 1, major)
        pair_sums(d)
        pair_copy(d).start()

    @pl.loop(1, major)
    def _(d):
        load(d, 0).wait()
        sums = packed_sums((ahead(d) * 2 + b) * group)
        pair_copy(d).wait_recv()
        for j in range(group):
            sums_out[d - 1, part(j)] = sums[j] + pair_in[d, part(j)]
        sum_copy(d).start()

    load(0, 0).wait()
    own = packed_sums(me * group)
    pair_copy(0).wait_recv()
    for j in range(group):
        own[j] = own[j] + pair_in[0, part(j)]
    for d in range(1, major):
        sum_copy(d).wait_recv()
        for j in range(group):
            own[j] = own[j] + sums_in[d - 1, part(j)]

    maps = polar_map([unpack(o) for o in own])
    for j in range(group):
        maps_out[part(j)] = pack(maps[j][:half])
    def take(d):
        first = (behind(d) * 2 + b) * group
        apply(held, first, [unpack(maps_in[d - 1, part(j)]) for j in range(group)], out, first)

    if major > 1:
        map_copy(via).start()
    for d in range(1, major):
        if d != via:
            cross_copy(d).start()
            map_copy(d).start()
    cross_copy(0).start()
    apply(held, me * group, maps, out, me * group)
    if major > 1:
        map_copy(via).wait_recv()
        cross_copy(via).start()
        take(via)

    @pl.loop(0, major - 2)
    def _(i):
        d = lax.rem(via + i, major - 1) + 1
        map_copy(d).wait_recv()
        take(d)

    cross_copy(0).wait_recv()
    first = partner * group
    apply(held, first, [unpack(maps_pair[0, part(j)]) for j in range(group)], out, first)
    for d in range(1, major):
        cross_copy(d).wait_recv()

    for d in range(major):
        pair_copy(d).wait_send()
        cross_copy(d).wait_send()
        if d > 0:
            sum_copy(d).wait_send()
            map_copy(d).wait_send()


def finish_kernel(n, shapes, held, maps_pair, out, late, early_sem, late_sem):
    major = n // 2
    me = lax.axis_index("pts")
    a, b = me // 2, lax.rem(me, 2)
    group = held.shape[0] // n
    quarter = maps_pair.shape[1] // group

    def early_copy(d):
        rows = pl.ds((lax.rem(a + major - d, major) * 2 + b) * group, group)
        return pltpu.make_async_copy(shapes.at[rows], out.at[rows], early_sem.at[d])

    def late_first(d):
        return (lax.rem(a + major - d, major) * 2 + 1 - b) * group

    def late_copy(d):
        return pltpu.make_async_copy(
            late.at[pl.ds((d - 1) * group, group)],
            out.at[pl.ds(late_first(d), group)],
            late_sem.at[d],
        )

    pair_rows = pl.ds(late_first(0), group)
    pair_copy = pltpu.make_async_copy(shapes.at[pair_rows], out.at[pair_rows], late_sem.at[0])
    for d in range(major):
        early_copy(d).start()
    pair_copy.start()

    @pl.loop(1, major)
    def _(d):
        maps = [unpack(maps_pair[d, pl.ds(j * quarter, quarter)]) for j in range(group)]
        apply(held, late_first(d), maps, late, (d - 1) * group)
        late_copy(d).start()

    for d in range(major):
        early_copy(d).wait()
    pair_copy.wait()
    for d in range(1, major):
        late_copy(d).wait()


def local(n, spectra, weights):
    freq_count, var_count, points, cols = spectra.shape
    block = (freq_count // n * (cols // 4), cols)
    major = n // 2
    dma = pltpu.SemaphoreType.DMA
    shapes, held, maps_pair = pl.pallas_call(
        functools.partial(main_kernel, n),
        out_shape=[
            jax.ShapeDtypeStruct(spectra.shape, jnp.bfloat16),
            jax.ShapeDtypeStruct(spectra.shape, jnp.bfloat16),
            jax.ShapeDtypeStruct((major, *block), jnp.float32),
        ],
        in_specs=[pl.BlockSpec(memory_space=pltpu.HBM)] * 2,
        out_specs=[pl.BlockSpec(memory_space=pltpu.VMEM)] * 3,
        scratch_shapes=[
            pltpu.VMEM((1, points), jnp.float32),
            pltpu.VMEM((points, cols), jnp.float32),
            pltpu.VMEM((major, *block), jnp.float32),
            pltpu.VMEM((major, *block), jnp.float32),
            pltpu.VMEM((major - 1, *block), jnp.float32),
            pltpu.VMEM((major - 1, *block), jnp.float32),
            pltpu.VMEM(block, jnp.float32),
            pltpu.VMEM((major - 1, *block), jnp.float32),
            dma((2, major)),
            dma,
            dma((major,)),
            dma((major,)),
            dma((major - 1,)),
            dma((major - 1,)),
            dma((major - 1,)),
            dma((major - 1,)),
            dma((major,)),
            dma((major,)),
        ],
        compiler_params=pltpu.CompilerParams(
            collective_id=0, has_side_effects=True, vmem_limit_bytes=32 * 1024 * 1024
        ),
        name="polar_shapes",
    )(
        pltpu.with_memory_space_constraint(spectra, pltpu.HBM),
        pltpu.with_memory_space_constraint(weights.reshape(1, points), pltpu.HBM),
    )
    return pl.pallas_call(
        functools.partial(finish_kernel, n),
        out_shape=jax.ShapeDtypeStruct(spectra.shape, jnp.bfloat16),
        in_specs=[pl.BlockSpec(memory_space=pltpu.VMEM)] * 3,
        out_specs=pl.BlockSpec(memory_space=pltpu.HBM),
        scratch_shapes=[
            pltpu.VMEM((max(1, freq_count // 2 - freq_count // n), *spectra.shape[1:]), jnp.bfloat16),
            dma((major,)),
            dma((major,)),
        ],
        compiler_params=pltpu.CompilerParams(vmem_limit_bytes=32 * 1024 * 1024),
        name="finish_shapes",
    )(shapes, held, maps_pair)


def solution(mesh):
    in_specs = (P("freq", None, "pts", None), P("pts"))
    out_specs = P("freq", None, "pts", None)
    return jax.shard_map(
        functools.partial(local, mesh.shape["pts"]),
        mesh=mesh, in_specs=in_specs, out_specs=out_specs, check_vma=False,
    )
```

```python
import functools

import jax
import jax.numpy as jnp
from jax import lax
from jax.experimental import pallas as pl
from jax.experimental.pallas import tpu as pltpu
from jax.sharding import PartitionSpec as P

NS_STEPS = 10
MESH = pl.DeviceIdType.MESH


def places(shape):
    return (
        lax.broadcasted_iota(jnp.int32, shape, 0),
        lax.broadcasted_iota(jnp.int32, shape, 1),
    )


def pack(top):
    half, cols = top.shape
    row, lane = places(top.shape)
    left = lane < half
    upper = jnp.where(left, lane, lane - half) >= row
    rolled = pltpu.roll(top, half, 1)
    both = jnp.where(jnp.logical_xor(left, upper), rolled, top)
    quarter = half // 2
    return jnp.where(left[:quarter], both[:quarter], both[quarter:])


def unpack(packed):
    quarter, cols = packed.shape
    half = 2 * quarter
    left = places(packed.shape)[1] < half
    rolled = pltpu.roll(packed, half, 1)
    top = jnp.where(left, packed, rolled)
    bottom = jnp.where(left, rolled, packed)
    full = jnp.concatenate([top, bottom, top, bottom], 0)
    flipped = full.T
    row, lane = places(full.shape)
    row_left, lane_left = row < half, lane < half
    i = jnp.where(row_left, row, row - half)
    j = jnp.where(lane_left, lane, lane - half)
    real = jnp.where(j >= i, full, flipped)
    imag = jnp.where(j < i, full, jnp.where(j > i, -flipped, 0.0))
    imag = jnp.where(row_left, imag, -imag)
    return jnp.where(jnp.logical_xor(row_left, lane_left), imag, real)


def split(a):
    high = a.astype(jnp.bfloat16)
    low = (a - high.astype(jnp.float32)).astype(jnp.bfloat16)
    return high, low


def left_form(a):
    return jnp.concatenate(split(a), 1)


def product(left, right):
    wide = jnp.dot(left, right, preferred_element_type=jnp.float32)
    cols = wide.shape[1] // 2
    return wide[:, :cols] + wide[:, cols:]


def polar_map(crosses):
    order = crosses[0].shape[0]
    row, lane = places((order, order))
    eye = row == lane
    traces = [jnp.sum(jnp.where(eye, c, 0.0), keepdims=True) for c in crosses]
    grams = [c / t for c, t in zip(crosses, traces)]
    maps = [jnp.where(eye, 1.5 - 0.5 * g, -0.5 * g) for g in grams]
    for step in range(NS_STEPS):
        lefts = [left_form(g) for g in grams]
        rights = [jnp.concatenate([g, g], 0) for g in lefts]
        if step == 0:
            squares = [product(g, r) for g, r in zip(lefts, rights)]
        elif step < NS_STEPS - 1:
            both = [
                product(jnp.concatenate([g, left_form(q)], 0), r)
                for g, q, r in zip(lefts, maps, rights)
            ]
            squares = [x[:order] for x in both]
            maps = [1.5 * q - 0.5 * x[order:] for q, x in zip(maps, both)]
        else:
            maps = [1.5 * q - 0.5 * product(left_form(q), r) for q, r in zip(maps, rights)]
        if step < NS_STEPS - 1:
            halves = [1.5 * g - 0.5 * x for g, x in zip(grams, squares)]
            grams = [
                1.5 * t - 0.5 * product(left_form(t), r) for t, r in zip(halves, rights)
            ]
    return [q * lax.rsqrt(t) for q, t in zip(maps, traces)]


def apply(held, first, maps, out, place):
    group = len(maps)
    _, var_count, points, cols = held.shape
    maps = [m.astype(jnp.bfloat16) for m in maps]
    if group == 2:
        zero = jnp.zeros((cols, cols), jnp.bfloat16)
        right = jnp.concatenate(
            [
                jnp.concatenate([maps[0], zero], 1),
                jnp.concatenate([zero, maps[1]], 1),
            ],
            0,
        )
        for v in range(var_count):
            left = jnp.concatenate([held[first, v], held[first + 1, v]], 1)
            wide = jnp.dot(left, right, preferred_element_type=jnp.float32).astype(out.dtype)
            out[place, v] = wide[:, :cols]
            out[place + 1, v] = wide[:, cols:]
    else:
        for j in range(group):
            for v in range(var_count):
                out[place + j, v] = jnp.dot(
                    held[first + j, v], maps[j], preferred_element_type=jnp.float32
                ).astype(out.dtype)


def main_kernel(
    n, spectra, weights, out, held, maps_pair, row_weights, root, pair_out, pair_in, sums_out,
    sums_in, maps_out, maps_in, load_sem, weight_sem, pair_send, pair_recv, sum_send, sum_recv,
    map_send, map_recv, cross_send, cross_recv,
):
    major = n // 2
    me = lax.axis_index("pts")
    a, b = me // 2, lax.rem(me, 2)
    other = 1 - b
    partner = a * 2 + other
    _, var_count, points, cols = held.shape
    group = held.shape[0] // n
    half = cols // 2
    quarter = half // 2

    def ahead(d):
        return lax.rem(a + d, major)

    def behind(d):
        return lax.rem(a + major - d, major)

    def load(d, side):
        start = (ahead(d) * 2 + (b if side == 0 else other)) * group
        rows = pl.ds(start, group)
        return pltpu.make_async_copy(spectra.at[rows], held.at[rows], load_sem.at[side, d])

    def send(src, dst, send_sem, recv_sem, target):
        return pltpu.make_async_remote_copy(
            src_ref=src, dst_ref=dst, send_sem=send_sem, recv_sem=recv_sem,
            device_id={"pts": target}, device_id_type=MESH,
        )

    def pair_copy(d):
        return send(pair_out.at[d], pair_in.at[d], pair_send.at[d], pair_recv.at[d], partner)

    def sum_copy(d):
        return send(
            sums_out.at[d - 1], sums_in.at[d - 1], sum_send.at[d - 1], sum_recv.at[d - 1],
            ahead(d) * 2 + b,
        )

    def map_copy(d):
        return send(
            maps_out, maps_in.at[d - 1], map_send.at[d - 1], map_recv.at[d - 1], ahead(d) * 2 + b
        )

    via = major // 2

    def cross_copy(d):
        src = maps_in.at[d - 1] if d == via and d > 0 else maps_out
        target = partner if d == via else ahead(d) * 2 + other
        return send(src, maps_pair.at[d], cross_send.at[d], cross_recv.at[d], target)

    barrier = pltpu.get_barrier_semaphore()
    pl.semaphore_signal(barrier, inc=1, device_id={"pts": partner}, device_id_type=MESH)
    for d in range(1, major):
        pl.semaphore_signal(
            barrier, inc=1, device_id={"pts": ahead(d) * 2 + b}, device_id_type=MESH
        )
    for d in range(1, major):
        if d != via:
            pl.semaphore_signal(
                barrier, inc=1, device_id={"pts": ahead(d) * 2 + other}, device_id_type=MESH
            )
    weight_copy = pltpu.make_async_copy(weights, row_weights, weight_sem)
    weight_copy.start()
    loads = [load(d % major, side) for side in (1, 0) for d in range(1, major + 1)]
    for copy in loads[:2]:
        copy.start()
    weight_copy.wait()
    root[...] = jnp.broadcast_to(jnp.sqrt(row_weights[...]), (cols, points)).T
    for copy in loads[2:]:
        copy.start()

    def fold(total):
        top, bottom = total[:half], pltpu.roll(total[half:], half, 1)
        lane = places(top.shape)[1]
        return pack(top + jnp.where(lane < half, bottom, -bottom))

    def packed_sums(first):
        sums = []
        for start in range(0, group, 2):
            count = min(2, group - start)
            rows = jnp.concatenate(
                [
                    (held[first + start + j].astype(jnp.float32) * root[...])
                    .astype(jnp.bfloat16)
                    .reshape(var_count * points, cols)
                    for j in range(count)
                ],
                1,
            )
            total = lax.dot_general(
                rows, rows, (((0,), (0,)), ((), ())), preferred_element_type=jnp.float32
            )
            for j in range(count):
                own_cols = slice(j * cols, (j + 1) * cols)
                sums.append(fold(total[own_cols, own_cols]))
        return sums

    def part(j):
        return pl.ds(j * quarter, quarter)

    def pair_sums(d):
        load(d, 1).wait()
        for j, packed in enumerate(packed_sums((ahead(d) * 2 + other) * group)):
            pair_out[d, part(j)] = packed

    early = min(2, major)

    @pl.loop(0, early)
    def _(i):
        pair_sums(lax.rem(i + 1, major))

    pl.semaphore_wait(barrier, major + max(major - 2, 0))
    for i in range(early):
        pair_copy((i + 1) % major).start()

    @pl.loop(early, major)
    def _(i):
        d = lax.rem(i + 1, major)
        pair_sums(d)
        pair_copy(d).start()

    @pl.loop(1, major)
    def _(d):
        load(d, 0).wait()
        sums = packed_sums((ahead(d) * 2 + b) * group)
        pair_copy(d).wait_recv()
        for j in range(group):
            sums_out[d - 1, part(j)] = sums[j] + pair_in[d, part(j)]
        sum_copy(d).start()

    load(0, 0).wait()
    own = packed_sums(me * group)
    pair_copy(0).wait_recv()
    for j in range(group):
        own[j] = own[j] + pair_in[0, part(j)]
    for d in range(1, major):
        sum_copy(d).wait_recv()
        for j in range(group):
            own[j] = own[j] + sums_in[d - 1, part(j)]

    maps = polar_map([unpack(o) for o in own])
    for j in range(group):
        maps_out[part(j)] = pack(maps[j][:half])
    def take(d):
        first = (behind(d) * 2 + b) * group
        apply(held, first, [unpack(maps_in[d - 1, part(j)]) for j in range(group)], out, first)

    if major > 1:
        map_copy(via).start()
    for d in range(1, major):
        if d != via:
            cross_copy(d).start()
            map_copy(d).start()
    cross_copy(0).start()
    apply(held, me * group, maps, out, me * group)
    if major > 1:
        map_copy(via).wait_recv()
        cross_copy(via).start()
        take(via)

    @pl.loop(0, major - 2)
    def _(i):
        d = lax.rem(via + i, major - 1) + 1
        map_copy(d).wait_recv()
        take(d)

    cross_copy(0).wait_recv()
    first = partner * group
    apply(held, first, [unpack(maps_pair[0, part(j)]) for j in range(group)], out, first)
    for d in range(1, major):
        cross_copy(d).wait_recv()

    for d in range(major):
        pair_copy(d).wait_send()
        cross_copy(d).wait_send()
        if d > 0:
            sum_copy(d).wait_send()
            map_copy(d).wait_send()


def finish_kernel(n, shapes, held, maps_pair, out, late, early_sem, late_sem):
    major = n // 2
    me = lax.axis_index("pts")
    a, b = me // 2, lax.rem(me, 2)
    group = held.shape[0] // n
    quarter = maps_pair.shape[1] // group

    def early_copy(d):
        rows = pl.ds((lax.rem(a + major - d, major) * 2 + b) * group, group)
        return pltpu.make_async_copy(shapes.at[rows], out.at[rows], early_sem.at[d])

    def late_first(d):
        return (lax.rem(a + major - d, major) * 2 + 1 - b) * group

    def late_copy(d):
        return pltpu.make_async_copy(
            late.at[pl.ds((d - 1) * group, group)],
            out.at[pl.ds(late_first(d), group)],
            late_sem.at[d],
        )

    pair_rows = pl.ds(late_first(0), group)
    pair_copy = pltpu.make_async_copy(shapes.at[pair_rows], out.at[pair_rows], late_sem.at[0])
    for d in range(major):
        early_copy(d).start()
    pair_copy.start()

    @pl.loop(1, major)
    def _(d):
        maps = [unpack(maps_pair[d, pl.ds(j * quarter, quarter)]) for j in range(group)]
        apply(held, late_first(d), maps, late, (d - 1) * group)
        late_copy(d).start()

    for d in range(major):
        early_copy(d).wait()
    pair_copy.wait()
    for d in range(1, major):
        late_copy(d).wait()


def local(n, spectra, weights):
    freq_count, var_count, points, cols = spectra.shape
    block = (freq_count // n * (cols // 4), cols)
    major = n // 2
    dma = pltpu.SemaphoreType.DMA
    shapes, held, maps_pair = pl.pallas_call(
        functools.partial(main_kernel, n),
        out_shape=[
            jax.ShapeDtypeStruct(spectra.shape, jnp.bfloat16),
            jax.ShapeDtypeStruct(spectra.shape, jnp.bfloat16),
            jax.ShapeDtypeStruct((major, *block), jnp.float32),
        ],
        in_specs=[pl.BlockSpec(memory_space=pltpu.HBM)] * 2,
        out_specs=[pl.BlockSpec(memory_space=pltpu.VMEM)] * 3,
        scratch_shapes=[
            pltpu.VMEM((1, points), jnp.float32),
            pltpu.VMEM((points, cols), jnp.float32),
            pltpu.VMEM((major, *block), jnp.float32),
            pltpu.VMEM((major, *block), jnp.float32),
            pltpu.VMEM((major - 1, *block), jnp.float32),
            pltpu.VMEM((major - 1, *block), jnp.float32),
            pltpu.VMEM(block, jnp.float32),
            pltpu.VMEM((major - 1, *block), jnp.float32),
            dma((2, major)),
            dma,
            dma((major,)),
            dma((major,)),
            dma((major - 1,)),
            dma((major - 1,)),
            dma((major - 1,)),
            dma((major - 1,)),
            dma((major,)),
            dma((major,)),
        ],
        compiler_params=pltpu.CompilerParams(
            collective_id=0, has_side_effects=True, vmem_limit_bytes=32 * 1024 * 1024
        ),
        name="polar_shapes",
    )(
        pltpu.with_memory_space_constraint(spectra, pltpu.HBM),
        pltpu.with_memory_space_constraint(weights.reshape(1, points), pltpu.HBM),
    )
    return pl.pallas_call(
        functools.partial(finish_kernel, n),
        out_shape=jax.ShapeDtypeStruct(spectra.shape, jnp.bfloat16),
        in_specs=[pl.BlockSpec(memory_space=pltpu.VMEM)] * 3,
        out_specs=pl.BlockSpec(memory_space=pltpu.HBM),
        scratch_shapes=[
            pltpu.VMEM((max(1, freq_count // 2 - freq_count // n), *spectra.shape[1:]), jnp.bfloat16),
            dma((major,)),
            dma((major,)),
        ],
        compiler_params=pltpu.CompilerParams(vmem_limit_bytes=32 * 1024 * 1024),
        name="finish_shapes",
    )(shapes, held, maps_pair)


def solution(mesh):
    in_specs = (P("freq", None, "pts", None), P("pts"))
    out_specs = P("freq", None, "pts", None)
    return jax.shard_map(
        functools.partial(local, mesh.shape["pts"]),
        mesh=mesh, in_specs=in_specs, out_specs=out_specs, check_vma=False,
    )
```
